512 devices in a mesh: tp: 8 (over y, core), ad: 64 (over z, x).
Axes of the slice: x: 4, y: 4, z: 16, core: 2. Of those that a mesh axis runs over, the one named last changes fastest.
Arguments:
- tokens: bfloat16 [16384, 4096], P('ad', 'tp'), may hold values from -6 to 6
- key_value_weight: bfloat16 [4096, 2048], P('tp'), may hold values from -0.09375 to 0.09375
- adapter_down_weight: bfloat16 [512, 32, 4096], P('ad', None, 'tp'), may hold values from -0.09375 to 0.09375
- adapter_up_weight: bfloat16 [512, 16, 2048], P('ad', None, 'tp'), may hold values from -1.5 to 1.5
- request_adapter_index: int32 [4096], P('ad'), may hold values from 0 to 511, as said below
- lengths: int32 [64, 64], P('ad'), may hold values from 1 to 8, 256 in all within a row
Outputs:
- mixed: bfloat16 [16384, 2048], P('ad', 'tp')
The draws below stay inside these ranges and needn't reach their ends.
Inputs may be any that keep to these rules, and one draw needn't show every extreme that they name: `request_adapter_index`: owner o stores adapters o * 8 to (o+1) * 8 - 1. Among the 64 requests of one token group, the adapters of exactly one owner are named by exactly 2 requests and those of every other owner by at most one.
All inputs are finite; a program needn't handle non-finite values.
Results may differ from the reference program's by a relative error of at most 0.018.
Values may be sent and summed in bfloat16 or wider, within the bound.
No kernel may reach another device: no remote copies, remote signals or barrier semaphores. Data moves between devices by JAX's collectives and lax.ppermute only.
A program may use at most 64 MiB of HBM per device.

```python
import math
import jax
import jax.numpy as jnp
import numpy as np
from jax import lax

MODEL_WIDTH = 4096
KEY_VALUE_WIDTH = 1024
ADAPTER_RANK = 16
TOK_DEV = 256
ADP_DEV = 8
REQ_DEV = 64
MAXLEN = 8
TOKENS = 16384
ADAPTER_COUNT = 512
N_TP = 8
N_AD = 64


def draw_request_adapter_index(key, part):
    key = jax.random.fold_in(key, 17)

    def one_block(block_key):
        first, second, third = jax.random.split(block_key, 3)
        owners = jax.random.permutation(first, N_AD)
        picks = jnp.maximum(jnp.arange(REQ_DEV) - 1, 0)
        chosen = owners[picks]
        shuffled = chosen[jax.random.permutation(second, REQ_DEV)]
        inside = jax.random.randint(third, (REQ_DEV,), 0, ADP_DEV)
        return (shuffled * ADP_DEV + inside).astype(jnp.int32)
    return jax.vmap(one_block)(jax.random.split(key, N_AD)).reshape(-1).astype(jnp.int32)


def steps_of(stream_key, dims, shards, least, top_value):
    def one(position, shards_of):
        steps = jax.random.uniform(jax.random.fold_in(jax.random.fold_in(stream_key, 6), position), (shards_of,), jnp.float32, least / len(shards), top_value / len(shards))
        return jnp.repeat(jnp.exp(steps), dims[position] // shards_of).reshape((-1,) + (1,) * (len(dims) - position - 1))

    gain = one(*shards[0])
    for cut in shards[1:]:
        gain = gain * one(*cut)
    return gain


def length_profile(number_of, total, limit, lean):
    loads = [(1 << 20) // math.isqrt(standing ** lean) + 1 for standing in range(2, number_of + 1)]
    rest, given = total - limit - (number_of - 1), [1] * (number_of - 1)
    while rest > 0:
        candidates = [i for i in range(number_of - 1) if given[i] < limit]
        mass, remaining = sum([loads[i] for i in candidates]), rest
        for i in candidates:
            extra = min(limit - given[i], max(1, remaining * loads[i] // mass), rest)
            given[i] = given[i] + extra
            rest = rest - extra
    return np.array([limit] + given)


def uneven_parts(key, count, total, limit, skew):
    if count == 2:
        one = jax.random.randint(key, (), max(1, total - limit), min(limit, total - 1) + 1)
        return jnp.stack([one, total - one])
    tallies = jnp.asarray(length_profile(count, total, limit, skew), jnp.int32)
    pairs = (count - 1) // 2
    giver, receiver = tallies[1:1 + 2 * pairs:2], tallies[2:2 + 2 * pairs:2]
    margin = jnp.minimum(giver - 1, limit - receiver)
    moved = jax.random.randint(jax.random.fold_in(key, 1), (pairs,), 0, 1 << 20) % (margin + 1)
    tallies = tallies.at[1:1 + 2 * pairs:2].set(giver - moved).at[2:2 + 2 * pairs:2].set(receiver + moved)
    return tallies[jax.random.permutation(jax.random.fold_in(key, 2), count)]


def bell_draw(key, dims, spread, bound, cuts=(), kind=jnp.bfloat16):
    result = spread * jax.random.normal(key, dims, jnp.float32)
    if cuts:
        result = result * steps_of(key, dims, cuts, -0.22, 0.18)
    return jnp.clip(result, -bound, bound).astype(kind)


def setup_inputs(seed: int = 0) -> dict:
    arg_keys = jax.random.split(jax.random.key(seed), 7)
    return {
        "tokens": bell_draw(arg_keys[0], (TOKENS, MODEL_WIDTH), 1.0, 6.0, ((0, 64), (1, 8))),
        "key_value_weight": bell_draw(arg_keys[1], (MODEL_WIDTH, 2 * KEY_VALUE_WIDTH), MODEL_WIDTH ** -0.5, 0.09375, ((0, 8),)),
        "adapter_down_weight": bell_draw(arg_keys[2], (ADAPTER_COUNT, 2 * ADAPTER_RANK, MODEL_WIDTH), MODEL_WIDTH ** -0.5, 0.09375, ((0, 64), (2, 8))),
        "adapter_up_weight": bell_draw(arg_keys[3], (ADAPTER_COUNT, ADAPTER_RANK, 2 * KEY_VALUE_WIDTH), ADAPTER_RANK ** -0.5, 1.5, ((0, 64), (2, 8))),
        "request_adapter_index": draw_request_adapter_index(jax.random.fold_in(arg_keys[6], 71), 0),
        "lengths": jax.vmap(lambda own: uneven_parts(own, REQ_DEV, TOK_DEV, MAXLEN, 2))(jax.random.split(arg_keys[5], N_AD)).reshape((N_AD, REQ_DEV)).astype(jnp.int32),
    }


ADAPTER_SCALE = 2.0


def reference(tokens, key_value_weight, adapter_down_weight, adapter_up_weight, request_adapter_index, lengths):
    width = MODEL_WIDTH // N_TP
    base_output = jnp.zeros((TOKENS, 2 * KEY_VALUE_WIDTH), jnp.float32)
    for part in range(N_TP):
        piece = jnp.dot(tokens[:, part * width:(part + 1) * width], key_value_weight[part * width:(part + 1) * width], preferred_element_type=jnp.float32)
        rounded = lax.optimization_barrier(piece.astype(jnp.bfloat16))
        base_output = base_output + rounded.astype(jnp.float32)

    def one_group(block):
        rows, adapter_index, lens = block
        ends = jnp.cumsum(lens).astype(jnp.int32)
        starts = (ends - lens).astype(jnp.int32)
        offsets = jnp.arange(MAXLEN, dtype=jnp.int32)
        live = offsets[None, :] < lens[:, None]
        take = jnp.where(live, starts[:, None] + offsets[None, :], 0).astype(jnp.int32)
        padded = jnp.where(live[:, :, None], rows[take].astype(jnp.float32), jnp.float32(0.0))
        down_factor = adapter_down_weight[adapter_index].astype(jnp.float32)
        low = jnp.einsum("rmd,rcd->rmc", padded, down_factor, precision=lax.Precision.HIGHEST)
        up_factor = adapter_up_weight[adapter_index].astype(jnp.float32)
        delta_keys = jnp.einsum("rmc,rck->rmk", low[:, :, :ADAPTER_RANK], up_factor[:, :, :KEY_VALUE_WIDTH], precision=lax.Precision.HIGHEST)
        delta_values = jnp.einsum("rmc,rck->rmk", low[:, :, ADAPTER_RANK:], up_factor[:, :, KEY_VALUE_WIDTH:], precision=lax.Precision.HIGHEST)
        adapter_delta = jnp.concatenate([delta_keys, delta_values], axis=2).reshape(REQ_DEV * MAXLEN, 2 * KEY_VALUE_WIDTH)
        positions = jnp.arange(TOK_DEV, dtype=jnp.int32)
        request_of = jnp.sum((positions[:, None] >= ends[None, :]).astype(jnp.int32), axis=1).astype(jnp.int32)
        inner = positions - starts[request_of]
        return adapter_delta[(request_of * MAXLEN + inner).astype(jnp.int32)]

    groups = (tokens.reshape(N_AD, TOK_DEV, MODEL_WIDTH), request_adapter_index.reshape(N_AD, REQ_DEV), lengths)
    adapter_delta = lax.map(one_group, groups).reshape(TOKENS, 2 * KEY_VALUE_WIDTH)
    return (base_output + ADAPTER_SCALE * adapter_delta).astype(jnp.bfloat16)
```

```python
import jax
import jax.numpy as jnp
from jax import lax
from jax.experimental import pallas as pl
from jax.experimental.pallas import tpu as pltpu
from jax.sharding import PartitionSpec as P

ADAPTER_SCALE = 2.0
N_X = 4
MAXLEN = 8

F32 = jnp.float32
BF16 = jnp.bfloat16
NT = (((1,), (1,)), ((), ()))
TN = (((0,), (0,)), ((), ()))
VMEM_LIMIT = 48 * 1024 * 1024


def iota(shape, dimension):
    return lax.broadcasted_iota(jnp.int32, shape, dimension)


def pack_kernel(planes, cap, per_plane, lens_ref, index_ref, tokens_ref, send_ref, ids_ref, place_ref):
    requests = lens_ref.shape[1]
    rows = tokens_ref.shape[0]
    lens = lens_ref[...].astype(F32)
    index = index_ref[...].astype(F32)
    r0, r1 = iota((requests, requests), 0), iota((requests, requests), 1)
    ends = jnp.sum(jnp.where(r1 <= r0, lens, 0.0), axis=1, keepdims=True)
    starts = jnp.sum(jnp.where(r1 < r0, lens, 0.0), axis=1, keepdims=True)
    index_col = jnp.sum(jnp.where(r1 == r0, index, 0.0), axis=1, keepdims=True)
    t = iota((requests, rows), 1).astype(F32)
    inside = (t >= starts) & (t < ends)
    adapter = jnp.sum(jnp.where(inside, index_col, 0.0), axis=0, keepdims=True)
    plane = jnp.floor(adapter * (1.0 / per_plane))
    local = adapter - plane * per_plane
    member = iota((planes, rows), 0).astype(F32) == plane
    before = (iota((rows, rows), 0) < iota((rows, rows), 1)).astype(F32).astype(BF16)
    counts = jnp.dot(member.astype(F32).astype(BF16), before, preferred_element_type=F32)
    rank = jnp.sum(jnp.where(member, counts, 0.0), axis=0, keepdims=True)
    place = (plane * cap + rank).astype(jnp.int32)
    select = (iota((planes * cap, rows), 0) == place).astype(F32).astype(BF16)
    send_ref[...] = jnp.dot(select, tokens_ref[...], preferred_element_type=F32).astype(BF16)
    at_rank = (iota((ids_ref.shape[1], rows), 0).astype(F32) == rank).astype(F32).astype(BF16)
    ids_ref[...] = lax.dot_general(
        jnp.where(member, local, 0.0).astype(BF16), at_rank, NT, preferred_element_type=F32
    )
    place_ref[...] = jnp.broadcast_to(place, place_ref.shape)


def low_kernel(planes, cap, recv_ref, ids_ref, down_ref, out_ref, lane_ids_ref):
    rows = recv_ref.shape[0]
    doubled_rank = down_ref.shape[1]
    slot = ids_ref.shape[1]
    source = iota((planes, rows), 0)
    p = iota((planes, rows), 1)
    mine = (p >= source * cap) & (p < source * cap + cap)
    offset = jnp.sum(jnp.where(mine, p - source * cap, 0).astype(F32), axis=0, keepdims=True)
    spread = (iota((slot, rows), 0).astype(F32) == offset).astype(F32).astype(BF16)
    ids = jnp.dot(ids_ref[...].astype(BF16), spread, preferred_element_type=F32)
    ids = jnp.sum(jnp.where(mine, ids, 0.0), axis=0, keepdims=True)
    lane_ids_ref[...] = jnp.broadcast_to(ids, lane_ids_ref.shape)
    recv = recv_ref[...]
    adapters = down_ref.shape[0]
    step = 8
    low = jnp.zeros((doubled_rank, rows), F32)
    for first in range(0, adapters, step):
        block = down_ref[first : first + step].reshape(step * doubled_rank, -1)
        values = lax.dot_general(block, recv, NT, preferred_element_type=F32)
        for a in range(step):
            low = jnp.where(
                ids == float(first + a), values[a * doubled_rank : (a + 1) * doubled_rank], low
            )
    low = low.astype(BF16)
    n = out_ref.shape[0]
    rank = doubled_rank // 2
    for j in range(n):
        half = j * 2 // n
        out_ref[j] = low[half * rank : (half + 1) * rank]


def delta_kernel(parts_ref, lane_ids_ref, up_ref, out_ref):
    low = parts_ref[0].astype(F32)
    for j in range(1, parts_ref.shape[0]):
        low = low + parts_ref[j].astype(F32)
    ids = lane_ids_ref[0:1, :]
    adapters = up_ref.shape[0]
    spread = jnp.concatenate(
        [jnp.where(ids == float(a), low, 0.0).astype(BF16) for a in range(adapters)], axis=0
    )
    up = up_ref[...].reshape(spread.shape[0], -1)
    out_ref[...] = lax.dot_general(spread, up, TN, preferred_element_type=F32).astype(BF16)


def mix_kernel(place_ref, back_ref, base_ref, out_ref):
    rows = base_ref.shape[0]
    place = place_ref[0:1, :]
    select = (iota((back_ref.shape[0], rows), 0) == place).astype(F32).astype(BF16)
    delta = lax.dot_general(select, back_ref[...], TN, preferred_element_type=F32)
    out_ref[...] = (base_ref[...].astype(F32) + ADAPTER_SCALE * delta).astype(BF16)


def call(kernel, out_shape, *args):
    return pl.pallas_call(
        kernel,
        out_shape=out_shape,
        compiler_params=pltpu.CompilerParams(vmem_limit_bytes=VMEM_LIMIT),
    )(*args)


def local(
    tokens, key_value_weight, adapter_down_weight, adapter_up_weight, request_adapter_index, lengths
):
    tok_rows, width = tokens.shape
    n_ad = lax.axis_size("ad")
    n_tp = lax.axis_size("tp")
    n_z = n_ad // N_X
    stored, doubled_rank, _ = adapter_down_weight.shape
    columns = adapter_up_weight.shape[2]
    per_plane = stored * N_X
    cap = (N_X + 1) * MAXLEN
    rows = n_z * cap
    along_x = [[z * N_X + x for x in range(N_X)] for z in range(n_z)]
    along_z = [[z * N_X + x for z in range(n_z)] for x in range(N_X)]

    def pack(*refs):
        pack_kernel(n_z, cap, per_plane, *refs)

    def project(*refs):
        low_kernel(n_z, cap, *refs)

    down = lax.all_gather(adapter_down_weight, "ad", axis_index_groups=along_x, tiled=True)
    up = lax.all_gather(adapter_up_weight, "ad", axis_index_groups=along_x, tiled=True)
    send, ids, place = call(
        pack,
        (
            jax.ShapeDtypeStruct((rows, width), BF16),
            jax.ShapeDtypeStruct((n_z, 128), F32),
            jax.ShapeDtypeStruct((8, tok_rows), jnp.int32),
        ),
        lengths,
        request_adapter_index.reshape(1, -1),
        tokens,
    )
    ids = lax.all_to_all(ids, "ad", 0, 0, axis_index_groups=along_z, tiled=True)
    recv = lax.all_to_all(
        send.reshape(n_z, cap, width), "ad", 0, 0, axis_index_groups=along_z, tiled=True
    )
    partial_value = jnp.dot(tokens, key_value_weight, preferred_element_type=F32)
    base = lax.psum_scatter(partial_value.astype(BF16), "tp", scatter_dimension=1, tiled=True)
    parts, lane_ids = call(
        project,
        (
            jax.ShapeDtypeStruct((n_tp, doubled_rank // 2, rows), BF16),
            jax.ShapeDtypeStruct((8, rows), F32),
        ),
        recv.reshape(rows, width),
        ids,
        down,
    )
    parts = lax.all_to_all(parts, "tp", 0, 0, tiled=True)
    delta = call(delta_kernel, jax.ShapeDtypeStruct((rows, columns), BF16), parts, lane_ids, up)
    back = lax.all_to_all(
        delta.reshape(n_z, cap, columns), "ad", 0, 0, axis_index_groups=along_z, tiled=True
    )
    return call(
        mix_kernel,
        jax.ShapeDtypeStruct((tok_rows, columns), BF16),
        place,
        back.reshape(rows, columns),
        base,
    )


def solution(mesh):
    return jax.shard_map(
        local,
        mesh=mesh,
        in_specs=(
            P("ad", "tp"),
            P("tp", None),
            P("ad", None, "tp"),
            P("ad", None, "tp"),
            P("ad"),
            P("ad", None),
        ),
        out_specs=P("ad", "tp"),
        check_vma=False,
    )
```

```python
import jax
import jax.numpy as jnp
from jax import lax
from jax.experimental import pallas as pl
from jax.experimental.pallas import tpu as pltpu
from jax.sharding import PartitionSpec as P

ADAPTER_SCALE = 2.0
N_X = 4
MAXLEN = 8

F32 = jnp.float32
BF16 = jnp.bfloat16
NT = (((1,), (1,)), ((), ()))
TN = (((0,), (0,)), ((), ()))
LANES = 128
VMEM_LIMIT = 48 * 1024 * 1024


def iota(shape, dimension):
    return lax.broadcasted_iota(jnp.int32, shape, dimension)


def pack_kernel(
    planes, cap, per_plane,
    lens_ref, index_ref, tokens_ref, down_ref, up_ref,
    send_ref, place_ref, factors_ref,
):
    requests = lens_ref.shape[1]
    rows, width = tokens_ref.shape
    rank, columns = up_ref.shape[1:]
    doubled = down_ref.shape[1]
    factors_ref[:, :doubled, :] = down_ref[...]
    for half in range(2):
        factors_ref[:, doubled:, half * columns : (half + 1) * columns] = up_ref[
            :, half * rank // 2 : (half + 1) * rank // 2, :
        ]
    lens = lens_ref[...].astype(F32)
    index = index_ref[...].astype(F32)
    r0, r1 = iota((requests, requests), 0), iota((requests, requests), 1)
    ends = jnp.sum(jnp.where(r1 <= r0, lens, 0.0), axis=1, keepdims=True)
    starts = jnp.sum(jnp.where(r1 < r0, lens, 0.0), axis=1, keepdims=True)
    index_col = jnp.sum(jnp.where(r1 == r0, index, 0.0), axis=1, keepdims=True)
    t = iota((requests, rows), 1).astype(F32)
    inside = (t >= starts) & (t < ends)
    adapter = jnp.sum(jnp.where(inside, index_col, 0.0), axis=0, keepdims=True)
    plane = jnp.floor(adapter * (1.0 / per_plane))
    local = adapter - plane * per_plane
    member = iota((planes, rows), 0).astype(F32) == plane
    before = (iota((rows, rows), 0) < iota((rows, rows), 1)).astype(F32).astype(BF16)
    counts = jnp.dot(member.astype(F32).astype(BF16), before, preferred_element_type=F32)
    rank_in = jnp.sum(jnp.where(member, counts, 0.0), axis=0, keepdims=True)
    place = (plane * cap + rank_in).astype(jnp.int32)
    place_ref[...] = jnp.broadcast_to(place, place_ref.shape)
    select = (iota((planes * cap, rows), 0) == place).astype(F32).astype(BF16)
    packed = jnp.dot(select, tokens_ref[...], preferred_element_type=F32)
    blocks = width // LANES
    for c in range(blocks):
        block = packed[:, c * LANES : (c + 1) * LANES].reshape(planes, cap, LANES)
        send_ref[:, c * cap : (c + 1) * cap, :] = block.astype(BF16)
    at_rank = (iota((LANES, rows), 0).astype(F32) == rank_in).astype(F32).astype(BF16)
    ids = lax.dot_general(
        jnp.where(member, local, 0.0).astype(BF16), at_rank, NT, preferred_element_type=F32
    )
    ids = jnp.broadcast_to(ids.reshape(planes, 1, LANES), (planes, 8, LANES))
    send_ref[:, blocks * cap :, :] = ids.astype(BF16)


def low_kernel(planes, cap, recv_ref, factors_ref, out_ref, lane_ids_ref):
    rows = planes * cap
    blocks = recv_ref.shape[1] // cap
    source = iota((planes, rows), 0)
    p = iota((planes, rows), 1)
    mine = (p >= source * cap) & (p < source * cap + cap)
    offset = jnp.sum(jnp.where(mine, p - source * cap, 0).astype(F32), axis=0, keepdims=True)
    spread = (iota((LANES, rows), 0).astype(F32) == offset).astype(F32).astype(BF16)
    ids = recv_ref[:, blocks * cap :, :].astype(F32)[:, 0, :].astype(BF16)
    ids = jnp.dot(ids, spread, preferred_element_type=F32)
    ids = jnp.sum(jnp.where(mine, ids, 0.0), axis=0, keepdims=True)
    lane_ids_ref[...] = jnp.broadcast_to(ids, lane_ids_ref.shape)
    recv = jnp.concatenate(
        [
            recv_ref[:, c * cap : (c + 1) * cap, :].astype(F32).reshape(rows, LANES).astype(BF16)
            for c in range(blocks)
        ],
        axis=1,
    )
    adapters = factors_ref.shape[0]
    n, rank = out_ref.shape[:2]
    doubled = 2 * rank
    step = 8
    low = jnp.zeros((doubled, rows), F32)
    for first in range(0, adapters, step):
        block = factors_ref[first : first + step, :doubled, :].reshape(step * doubled, -1)
        values = lax.dot_general(block, recv, NT, preferred_element_type=F32)
        for a in range(step):
            low = jnp.where(
                ids == float(first + a), values[a * doubled : (a + 1) * doubled], low
            )
    low = low.astype(BF16)
    for j in range(n):
        half = j * 2 // n
        out_ref[j] = low[half * rank : (half + 1) * rank]


def delta_kernel(parts_ref, lane_ids_ref, factors_ref, out_ref):
    low = parts_ref[0].astype(F32)
    for j in range(1, parts_ref.shape[0]):
        low = low + parts_ref[j].astype(F32)
    rank = low.shape[0]
    columns = out_ref.shape[1]
    ids = lane_ids_ref[0:1, :]
    adapters = factors_ref.shape[0]
    total = None
    for half in range(2):
        part = low[half * rank // 2 : (half + 1) * rank // 2]
        spread = jnp.concatenate(
            [jnp.where(ids == float(a), part, 0.0) for a in range(adapters)], axis=0
        ).astype(BF16)
        up = factors_ref[:, 2 * rank :, half * columns : (half + 1) * columns].astype(F32)
        up = up.reshape(spread.shape[0], columns).astype(BF16)
        product = lax.dot_general(spread, up, TN, preferred_element_type=F32)
        total = product if total is None else total + product
    out_ref[...] = total.astype(BF16)


def mix_kernel(place_ref, back_ref, base_ref, out_ref):
    rows = base_ref.shape[0]
    place = place_ref[0:1, :]
    select = (iota((back_ref.shape[0], rows), 0) == place).astype(F32).astype(BF16)
    delta = lax.dot_general(select, back_ref[...], TN, preferred_element_type=F32)
    out_ref[...] = (base_ref[...].astype(F32) + ADAPTER_SCALE * delta).astype(BF16)


def call(kernel, out_shape, *args):
    return pl.pallas_call(
        kernel,
        out_shape=out_shape,
        compiler_params=pltpu.CompilerParams(vmem_limit_bytes=VMEM_LIMIT),
    )(*args)


def local(
    tokens, key_value_weight, adapter_down_weight, adapter_up_weight, request_adapter_index, lengths
):
    tok_rows, width = tokens.shape
    n_ad = lax.axis_size("ad")
    n_tp = lax.axis_size("tp")
    n_z = n_ad // N_X
    stored, doubled_rank, _ = adapter_down_weight.shape
    columns = adapter_up_weight.shape[2]
    per_plane = stored * N_X
    cap = (N_X + 1) * MAXLEN
    rows = n_z * cap
    along_x = [[z * N_X + x for x in range(N_X)] for z in range(n_z)]
    along_z = [[z * N_X + x for z in range(n_z)] for x in range(N_X)]

    def pack(*refs):
        pack_kernel(n_z, cap, per_plane, *refs)

    def project(*refs):
        low_kernel(n_z, cap, *refs)

    send, place, factors = call(
        pack,
        (
            jax.ShapeDtypeStruct((n_z, width // LANES * cap + 8, LANES), BF16),
            jax.ShapeDtypeStruct((8, tok_rows), jnp.int32),
            jax.ShapeDtypeStruct((stored, doubled_rank + 8, width), BF16),
        ),
        lengths,
        request_adapter_index.reshape(1, -1),
        tokens,
        adapter_down_weight,
        adapter_up_weight,
    )
    factors = lax.all_gather(factors, "ad", axis_index_groups=along_x, tiled=True)
    recv = lax.all_to_all(send, "ad", 0, 0, axis_index_groups=along_z, tiled=True)
    partial_value = jnp.dot(tokens, key_value_weight, preferred_element_type=F32)
    base = lax.psum_scatter(partial_value.astype(BF16), "tp", scatter_dimension=1, tiled=True)
    parts, lane_ids = call(
        project,
        (
            jax.ShapeDtypeStruct((n_tp, doubled_rank // 2, rows), BF16),
            jax.ShapeDtypeStruct((8, rows), F32),
        ),
        recv,
        factors,
    )
    parts = lax.all_to_all(parts, "tp", 0, 0, tiled=True)
    delta = call(delta_kernel, jax.ShapeDtypeStruct((rows, columns), BF16), parts, lane_ids, factors)
    back = lax.all_to_all(
        delta.reshape(n_z, cap, columns), "ad", 0, 0, axis_index_groups=along_z, tiled=True
    )
    return call(
        mix_kernel,
        jax.ShapeDtypeStruct((tok_rows, columns), BF16),
        place,
        back.reshape(rows, columns),
        base,
    )


def solution(mesh):
    return jax.shard_map(
        local,
        mesh=mesh,
        in_specs=(
            P("ad", "tp"),
            P("tp", None),
            P("ad", None, "tp"),
            P("ad", None, "tp"),
            P("ad"),
            P("ad", None),
        ),
        out_specs=P("ad", "tp"),
        check_vma=False,
    )
```

```python
import jax
import jax.numpy as jnp
from jax import lax
from jax.experimental import pallas as pl
from jax.experimental.pallas import tpu as pltpu
from jax.sharding import PartitionSpec as P

ADAPTER_SCALE = 2.0
N_X = 4
MAXLEN = 8

F32 = jnp.float32
BF16 = jnp.bfloat16
NT = (((1,), (1,)), ((), ()))
TN = (((0,), (0,)), ((), ()))
LANES = 128
VMEM_LIMIT = 48 * 1024 * 1024


def iota(shape, dimension):
    return lax.broadcasted_iota(jnp.int32, shape, dimension)


def pack_kernel(
    planes, cap, per_plane,
    lens_hbm, index_hbm, tokens_hbm, down_hbm, up_hbm,
    send_ref, place_ref, factors_hbm,
    lens_ref, index_ref, tokens_ref, block_ref, up_ref, sems,
):
    requests = lens_ref.shape[1]
    rows, width = tokens_ref.shape
    adapters, rank, columns = up_ref.shape
    down_rows = down_hbm.shape[0]

    def copy(source, target, k):
        made = pltpu.make_async_copy(source, target, sems.at[k])
        made.start()
        return made

    get_lens = copy(lens_hbm, lens_ref, 0)
    get_index = copy(index_hbm, index_ref, 1)
    get_tokens = copy(tokens_hbm, tokens_ref, 2)
    get_down = copy(down_hbm, block_ref.at[pl.ds(0, down_rows)], 3)
    get_up = copy(up_hbm, up_ref, 4)

    get_lens.wait()
    get_index.wait()
    lens = lens_ref[...].astype(F32)
    index = index_ref[...].astype(F32)
    r0, r1 = iota((requests, requests), 0), iota((requests, requests), 1)
    ends = jnp.sum(jnp.where(r1 <= r0, lens, 0.0), axis=1, keepdims=True)
    starts = jnp.sum(jnp.where(r1 < r0, lens, 0.0), axis=1, keepdims=True)
    index_col = jnp.sum(jnp.where(r1 == r0, index, 0.0), axis=1, keepdims=True)
    t = iota((requests, rows), 1).astype(F32)
    inside = (t >= starts) & (t < ends)
    adapter = jnp.sum(jnp.where(inside, index_col, 0.0), axis=0, keepdims=True)
    plane = jnp.floor(adapter * (1.0 / per_plane))
    local = (adapter - plane * per_plane).astype(jnp.int32)
    my_x = lax.axis_index("ad") % N_X
    local = (local ^ (my_x * (per_plane // N_X))).astype(F32)
    member = iota((planes, rows), 0).astype(F32) == plane
    before = (iota((rows, rows), 0) < iota((rows, rows), 1)).astype(F32).astype(BF16)
    counts = jnp.dot(member.astype(F32).astype(BF16), before, preferred_element_type=F32)
    rank_in = jnp.sum(jnp.where(member, counts, 0.0), axis=0, keepdims=True)
    place = (plane * cap + rank_in).astype(jnp.int32)
    place_ref[...] = jnp.broadcast_to(place, place_ref.shape)
    select = (iota((planes * cap, rows), 0) == place).astype(F32).astype(BF16)

    get_up.wait()
    for a in range(adapters):
        pair, side = a // 2, a % 2
        block_ref[
            down_rows + pair * rank : down_rows + (pair + 1) * rank,
            side * columns : (side + 1) * columns,
        ] = up_ref[a]
    get_down.wait()
    put = copy(block_ref, factors_hbm, 5)

    get_tokens.wait()
    packed = jnp.dot(select, tokens_ref[...], preferred_element_type=F32)
    blocks = width // LANES
    for c in range(blocks):
        block = packed[:, c * LANES : (c + 1) * LANES].reshape(planes, cap, LANES)
        send_ref[:, c * cap : (c + 1) * cap, :] = block.astype(BF16)
    at_rank = (iota((LANES, rows), 0).astype(F32) == rank_in).astype(F32).astype(BF16)
    ids = lax.dot_general(
        jnp.where(member, local, 0.0).astype(BF16), at_rank, NT, preferred_element_type=F32
    )
    ids = jnp.broadcast_to(ids.reshape(planes, 1, LANES), (planes, 8, LANES))
    send_ref[:, blocks * cap :, :] = ids.astype(BF16)
    put.wait()


def base_kernel(place_ref, tokens_ref, weight_ref, keep_ref, send_ref):
    del place_ref
    columns = keep_ref.shape[2]
    me = lax.axis_index("tp")

    def block(relative):
        first = pl.multiple_of((me ^ relative) * columns, columns)
        return jnp.dot(
            tokens_ref[...], weight_ref[:, pl.ds(first, columns)], preferred_element_type=F32
        ).astype(BF16)

    for k, relative in enumerate((0, 6, 2, 4)):
        send_ref[k] = block(relative ^ 1)
        keep_ref[k] = block(relative)


def halve_kernel(keep_ref, recv_ref, kept_ref, send_ref):
    half = kept_ref.shape[0]
    for k in range(half):
        kept_ref[k] = keep_ref[k].astype(F32) + recv_ref[k].astype(F32)
        send_ref[k] = (keep_ref[half + k].astype(F32) + recv_ref[half + k].astype(F32)).astype(BF16)


def low_kernel(
    planes, cap, stored, recv_ref, f0_ref, f1_ref, f2_ref, f3_ref, kept_ref, out_ref, lane_ids_ref
):
    del kept_ref
    rows = planes * cap
    blocks = recv_ref.shape[1] // cap
    source = iota((planes, rows), 0)
    p = iota((planes, rows), 1)
    mine = (p >= source * cap) & (p < source * cap + cap)
    offset = jnp.sum(jnp.where(mine, p - source * cap, 0).astype(F32), axis=0, keepdims=True)
    spread = (iota((LANES, rows), 0).astype(F32) == offset).astype(F32).astype(BF16)
    ids = recv_ref[:, blocks * cap :, :].astype(F32)[:, 0, :].astype(BF16)
    ids = jnp.dot(ids, spread, preferred_element_type=F32)
    ids = jnp.sum(jnp.where(mine, ids, 0.0), axis=0, keepdims=True)
    lane_ids_ref[...] = jnp.broadcast_to(ids, lane_ids_ref.shape)
    recv = jnp.concatenate(
        [
            recv_ref[:, c * cap : (c + 1) * cap, :].astype(F32).reshape(rows, LANES).astype(BF16)
            for c in range(blocks)
        ],
        axis=1,
    )
    n, rank = out_ref.shape[:2]
    doubled = 2 * rank
    low = jnp.zeros((doubled, rows), F32)
    for x, factors_ref in enumerate((f0_ref, f1_ref, f2_ref, f3_ref)):
        block = factors_ref[: stored * doubled, :]
        values = lax.dot_general(block, recv, NT, preferred_element_type=F32)
        for a in range(stored):
            low = jnp.where(
                ids == float(x * stored + a), values[a * doubled : (a + 1) * doubled], low
            )
    low = low.astype(BF16)
    for j in range(n):
        half = j * 2 // n
        out_ref[j] = low[half * rank : (half + 1) * rank]


def delta_kernel(
    stored, parts_ref, lane_ids_ref, f0_ref, f1_ref, f2_ref, f3_ref, out_ref
):
    low = parts_ref[0].astype(F32)
    for j in range(1, parts_ref.shape[0]):
        low = low + parts_ref[j].astype(F32)
    rank = low.shape[0]
    columns = out_ref.shape[1]
    ids = lane_ids_ref[0:1, :]
    spread, up = [], []
    for x, factors_ref in enumerate((f0_ref, f1_ref, f2_ref, f3_ref)):
        for side in range(2):
            up.append(factors_ref[stored * 2 * rank :, side * columns : (side + 1) * columns])
            for pair in range(stored // 2):
                a = float(x * stored + 2 * pair + side)
                spread.append(jnp.where(ids == a, low, 0.0).astype(BF16))
    product = lax.dot_general(
        jnp.concatenate(spread, axis=0), jnp.concatenate(up, axis=0), TN, preferred_element_type=F32
    )
    out_ref[...] = product.astype(BF16)


def mix_kernel(place_ref, back_ref, kept_ref, recv_ref, out_ref):
    rows = out_ref.shape[0]
    place = place_ref[0:1, :]
    select = (iota((back_ref.shape[0], rows), 0) == place).astype(F32).astype(BF16)
    delta = lax.dot_general(select, back_ref[...], TN, preferred_element_type=F32)
    base = kept_ref[0] + recv_ref[0].astype(F32)
    out_ref[...] = (base + ADAPTER_SCALE * delta).astype(BF16)


def call(kernel, out_shape, *args):
    return pl.pallas_call(
        kernel,
        out_shape=out_shape,
        compiler_params=pltpu.CompilerParams(vmem_limit_bytes=VMEM_LIMIT),
    )(*args)


def local(
    tokens, key_value_weight, adapter_down_weight, adapter_up_weight, request_adapter_index, lengths
):
    tok_rows, width = tokens.shape
    n_ad = lax.axis_size("ad")
    n_tp = lax.axis_size("tp")
    n_z = n_ad // N_X
    stored, doubled_rank, _ = adapter_down_weight.shape
    rank, columns = adapter_up_weight.shape[1:]
    per_plane = stored * N_X
    cap = (N_X + 1) * MAXLEN
    rows = n_z * cap
    along_x = [[z * N_X + x for x in range(N_X)] for z in range(n_z)]
    along_z = [[z * N_X + x for z in range(n_z)] for x in range(N_X)]

    def pack(*refs):
        pack_kernel(n_z, cap, per_plane, *refs)

    def project(*refs):
        low_kernel(n_z, cap, stored, *refs)

    def apply_up(*refs):
        delta_kernel(stored, *refs)

    hbm = pl.BlockSpec(memory_space=pltpu.HBM)
    vmem = pl.BlockSpec(memory_space=pltpu.VMEM)
    block_rows = stored * doubled_rank + stored // 2 * rank
    send, place, factors = pl.pallas_call(
        pack,
        out_shape=(
            jax.ShapeDtypeStruct((n_z, width // LANES * cap + 8, LANES), BF16),
            jax.ShapeDtypeStruct((8, tok_rows), jnp.int32),
            jax.ShapeDtypeStruct((block_rows, width), BF16),
        ),
        in_specs=[hbm] * 5,
        out_specs=(vmem, vmem, hbm),
        scratch_shapes=[
            pltpu.VMEM((1, lengths.shape[1]), jnp.int32),
            pltpu.VMEM((1, lengths.shape[1]), jnp.int32),
            pltpu.VMEM((tok_rows, width), BF16),
            pltpu.VMEM((block_rows, width), BF16),
            pltpu.VMEM((stored, rank, columns), BF16),
            pltpu.SemaphoreType.DMA((6,)),
        ],
        compiler_params=pltpu.CompilerParams(vmem_limit_bytes=VMEM_LIMIT),
    )(
        lengths,
        request_adapter_index.reshape(1, -1),
        tokens,
        adapter_down_weight.reshape(stored * doubled_rank, width),
        adapter_up_weight,
    )
    recv = lax.all_to_all(send, "ad", 0, 0, axis_index_groups=along_z, tiled=True)
    factors = [factors] + [
        lax.ppermute(
            factors, "ad", [(z * N_X + x, z * N_X + (x ^ s)) for z in range(n_z) for x in range(N_X)]
        )
        for s in range(1, N_X)
    ]

    def swap(array, mask):
        return lax.ppermute(array, "tp", [(j, j ^ mask) for j in range(n_tp)])

    def blocks(count, kind):
        return jax.ShapeDtypeStruct((count, tok_rows, columns), kind)

    keep, out = call(base_kernel, (blocks(4, BF16), blocks(4, BF16)), place, tokens, key_value_weight)
    keep, out = call(halve_kernel, (blocks(2, F32), blocks(2, BF16)), keep, swap(out, 1))
    keep, out = call(halve_kernel, (blocks(1, F32), blocks(1, BF16)), keep, swap(out, 2))
    base_recv = swap(out, 6)
    parts, lane_ids = call(
        project,
        (
            jax.ShapeDtypeStruct((n_tp, doubled_rank // 2, rows), BF16),
            jax.ShapeDtypeStruct((8, rows), F32),
        ),
        recv,
        *factors,
        base_recv,
    )
    parts = lax.all_to_all(parts, "tp", 0, 0, tiled=True)
    delta = call(apply_up, jax.ShapeDtypeStruct((rows, columns), BF16), parts, lane_ids, *factors)
    back = lax.all_to_all(
        delta.reshape(n_z, cap, columns), "ad", 0, 0, axis_index_groups=along_z, tiled=True
    )
    return call(
        mix_kernel,
        jax.ShapeDtypeStruct((tok_rows, columns), BF16),
        place,
        back.reshape(rows, columns),
        keep,
        base_recv,
    )


def solution(mesh):
    return jax.shard_map(
        local,
        mesh=mesh,
        in_specs=(
            P("ad", "tp"),
            P("tp", None),
            P("ad", None, "tp"),
            P("ad", None, "tp"),
            P("ad"),
            P("ad", None),
        ),
        out_specs=P("ad", "tp"),
        check_vma=False,
    )
```

```python
import jax
import jax.numpy as jnp
from jax import lax
from jax.experimental import pallas as pl
from jax.experimental.pallas import tpu as pltpu
from jax.sharding import PartitionSpec as P

ADAPTER_SCALE = 2.0
N_X = 4
MAXLEN = 8

F32 = jnp.float32
BF16 = jnp.bfloat16
NT = (((1,), (1,)), ((), ()))
TN = (((0,), (0,)), ((), ()))
LANES = 128
VMEM_LIMIT = 48 * 1024 * 1024


def iota(shape, dimension):
    return lax.broadcasted_iota(jnp.int32, shape, dimension)


def pack_kernel(
    planes, cap, per_plane,
    lens_hbm, index_hbm, tokens_hbm, down_hbm, up_hbm,
    send_ref, place_ref, factors_hbm,
    lens_ref, index_ref, tokens_ref, block_ref, up_ref, sems,
):
    requests = lens_ref.shape[1]
    rows, width = tokens_ref.shape
    adapters, rank, columns = up_ref.shape
    down_rows = down_hbm.shape[0]

    def copy(source, target, k):
        made = pltpu.make_async_copy(source, target, sems.at[k])
        made.start()
        return made

    get_lens = copy(lens_hbm, lens_ref, 0)
    get_index = copy(index_hbm, index_ref, 1)
    get_tokens = copy(tokens_hbm, tokens_ref, 2)
    get_down = copy(down_hbm, block_ref.at[pl.ds(0, down_rows)], 3)
    get_up = copy(up_hbm, up_ref, 4)

    get_lens.wait()
    get_index.wait()
    lens = lens_ref[...].astype(F32)
    index = index_ref[...].astype(F32)
    r0, r1 = iota((requests, requests), 0), iota((requests, requests), 1)
    ends = jnp.sum(jnp.where(r1 <= r0, lens, 0.0), axis=1, keepdims=True)
    starts = jnp.sum(jnp.where(r1 < r0, lens, 0.0), axis=1, keepdims=True)
    index_col = jnp.sum(jnp.where(r1 == r0, index, 0.0), axis=1, keepdims=True)
    t = iota((requests, rows), 1).astype(F32)
    inside = (t >= starts) & (t < ends)
    adapter = jnp.sum(jnp.where(inside, index_col, 0.0), axis=0, keepdims=True)
    plane = jnp.floor(adapter * (1.0 / per_plane))
    local = (adapter - plane * per_plane).astype(jnp.int32)
    my_x = lax.axis_index("ad") % N_X
    local = (local ^ (my_x * (per_plane // N_X))).astype(F32)
    member = iota((planes, rows), 0).astype(F32) == plane
    before = (iota((rows, rows), 0) < iota((rows, rows), 1)).astype(F32).astype(BF16)
    counts = jnp.dot(member.astype(F32).astype(BF16), before, preferred_element_type=F32)
    rank_in = jnp.sum(jnp.where(member, counts, 0.0), axis=0, keepdims=True)
    place = (plane * cap + rank_in).astype(jnp.int32)
    place_ref[...] = jnp.broadcast_to(place, place_ref.shape)
    select = (iota((planes * cap, rows), 0) == place).astype(F32).astype(BF16)

    get_up.wait()
    for a in range(adapters):
        pair, side = a // 2, a % 2
        block_ref[
            down_rows + pair * rank : down_rows + (pair + 1) * rank,
            side * columns : (side + 1) * columns,
        ] = up_ref[a]
    get_down.wait()
    put = copy(block_ref, factors_hbm, 5)

    get_tokens.wait()
    packed = jnp.dot(select, tokens_ref[...], preferred_element_type=F32)
    blocks = width // LANES
    for c in range(blocks):
        block = packed[:, c * LANES : (c + 1) * LANES].reshape(planes, cap, LANES)
        send_ref[:, c * cap : (c + 1) * cap, :] = block.astype(BF16)
    at_rank = (iota((LANES, rows), 0).astype(F32) == rank_in).astype(F32).astype(BF16)
    ids = lax.dot_general(
        jnp.where(member, local, 0.0).astype(BF16), at_rank, NT, preferred_element_type=F32
    )
    ids = jnp.broadcast_to(ids.reshape(planes, 1, LANES), (planes, 8, LANES))
    send_ref[:, blocks * cap :, :] = ids.astype(BF16)
    put.wait()


def base_kernel(place_ref, tokens_ref, weight_ref, keep_ref, send_ref):
    del place_ref
    columns = keep_ref.shape[2]
    me = lax.axis_index("tp")

    def block(relative):
        first = pl.multiple_of((me ^ relative) * columns, columns)
        return jnp.dot(
            tokens_ref[...], weight_ref[:, pl.ds(first, columns)], preferred_element_type=F32
        ).astype(BF16)

    for k, relative in enumerate((0, 6, 2, 4)):
        send_ref[k] = block(relative ^ 1)
        keep_ref[k] = block(relative)


def halve_kernel(after_ref, keep_ref, recv_ref, kept_ref, send_ref):
    del after_ref
    half = kept_ref.shape[0]
    for k in range(half):
        kept_ref[k] = keep_ref[k].astype(F32) + recv_ref[k].astype(F32)
        send_ref[k] = (keep_ref[half + k].astype(F32) + recv_ref[half + k].astype(F32)).astype(BF16)


def low_kernel(
    planes, cap, stored, recv_ref, f0_ref, f1_ref, f2_ref, f3_ref, kept_ref, out_ref, lane_ids_ref
):
    del kept_ref
    rows = planes * cap
    blocks = recv_ref.shape[1] // cap
    source = iota((planes, rows), 0)
    p = iota((planes, rows), 1)
    mine = (p >= source * cap) & (p < source * cap + cap)
    offset = jnp.sum(jnp.where(mine, p - source * cap, 0).astype(F32), axis=0, keepdims=True)
    spread = (iota((LANES, rows), 0).astype(F32) == offset).astype(F32).astype(BF16)
    ids = recv_ref[:, blocks * cap :, :].astype(F32)[:, 0, :].astype(BF16)
    ids = jnp.dot(ids, spread, preferred_element_type=F32)
    ids = jnp.sum(jnp.where(mine, ids, 0.0), axis=0, keepdims=True)
    lane_ids_ref[...] = jnp.broadcast_to(ids, lane_ids_ref.shape)
    recv = jnp.concatenate(
        [
            recv_ref[:, c * cap : (c + 1) * cap, :].astype(F32).reshape(rows, LANES).astype(BF16)
            for c in range(blocks)
        ],
        axis=1,
    )
    n, rank = out_ref.shape[:2]
    doubled = 2 * rank
    low = jnp.zeros((doubled, rows), F32)
    for x, factors_ref in enumerate((f0_ref, f1_ref, f2_ref, f3_ref)):
        block = factors_ref[: stored * doubled, :]
        values = lax.dot_general(block, recv, NT, preferred_element_type=F32)
        for a in range(stored):
            low = jnp.where(
                ids == float(x * stored + a), values[a * doubled : (a + 1) * doubled], low
            )
    low = low.astype(BF16)
    for j in range(n):
        half = j * 2 // n
        out_ref[j] = low[half * rank : (half + 1) * rank]


def delta_kernel(
    stored, parts_ref, lane_ids_ref, f0_ref, f1_ref, f2_ref, f3_ref, out_ref, mark_ref
):
    low = parts_ref[0].astype(F32)
    for j in range(1, parts_ref.shape[0]):
        low = low + parts_ref[j].astype(F32)
    rank = low.shape[0]
    columns = out_ref.shape[1]
    ids = lane_ids_ref[0:1, :]
    spread, up = [], []
    for x, factors_ref in enumerate((f0_ref, f1_ref, f2_ref, f3_ref)):
        for side in range(2):
            up.append(factors_ref[stored * 2 * rank :, side * columns : (side + 1) * columns])
            for pair in range(stored // 2):
                a = float(x * stored + 2 * pair + side)
                spread.append(jnp.where(ids == a, low, 0.0).astype(BF16))
    product = lax.dot_general(
        jnp.concatenate(spread, axis=0), jnp.concatenate(up, axis=0), TN, preferred_element_type=F32
    )
    out_ref[...] = product.astype(BF16)
    mark_ref[...] = jnp.zeros(mark_ref.shape, F32)


def mix_kernel(place_ref, back_ref, kept_ref, recv_ref, out_ref):
    rows = out_ref.shape[0]
    place = place_ref[0:1, :]
    select = (iota((back_ref.shape[0], rows), 0) == place).astype(F32).astype(BF16)
    delta = lax.dot_general(select, back_ref[...], TN, preferred_element_type=F32)
    base = kept_ref[0] + recv_ref[0].astype(F32)
    out_ref[...] = (base + ADAPTER_SCALE * delta).astype(BF16)


def call(kernel, out_shape, *args):
    return pl.pallas_call(
        kernel,
        out_shape=out_shape,
        compiler_params=pltpu.CompilerParams(vmem_limit_bytes=VMEM_LIMIT),
    )(*args)


def local(
    tokens, key_value_weight, adapter_down_weight, adapter_up_weight, request_adapter_index, lengths
):
    tok_rows, width = tokens.shape
    n_ad = lax.axis_size("ad")
    n_tp = lax.axis_size("tp")
    n_z = n_ad // N_X
    stored, doubled_rank, _ = adapter_down_weight.shape
    rank, columns = adapter_up_weight.shape[1:]
    per_plane = stored * N_X
    cap = (N_X + 1) * MAXLEN
    rows = n_z * cap
    along_x = [[z * N_X + x for x in range(N_X)] for z in range(n_z)]
    along_z = [[z * N_X + x for z in range(n_z)] for x in range(N_X)]

    def pack(*refs):
        pack_kernel(n_z, cap, per_plane, *refs)

    def project(*refs):
        low_kernel(n_z, cap, stored, *refs)

    def apply_up(*refs):
        delta_kernel(stored, *refs)

    hbm = pl.BlockSpec(memory_space=pltpu.HBM)
    vmem = pl.BlockSpec(memory_space=pltpu.VMEM)
    block_rows = stored * doubled_rank + stored // 2 * rank
    send, place, factors = pl.pallas_call(
        pack,
        out_shape=(
            jax.ShapeDtypeStruct((n_z, width // LANES * cap + 8, LANES), BF16),
            jax.ShapeDtypeStruct((8, tok_rows), jnp.int32),
            jax.ShapeDtypeStruct((block_rows, width), BF16),
        ),
        in_specs=[hbm] * 5,
        out_specs=(vmem, vmem, hbm),
        scratch_shapes=[
            pltpu.VMEM((1, lengths.shape[1]), jnp.int32),
            pltpu.VMEM((1, lengths.shape[1]), jnp.int32),
            pltpu.VMEM((tok_rows, width), BF16),
            pltpu.VMEM((block_rows, width), BF16),
            pltpu.VMEM((stored, rank, columns), BF16),
            pltpu.SemaphoreType.DMA((6,)),
        ],
        compiler_params=pltpu.CompilerParams(vmem_limit_bytes=VMEM_LIMIT),
    )(
        *(
            pltpu.with_memory_space_constraint(array, pltpu.HBM)
            for array in (
                lengths,
                request_adapter_index.reshape(1, -1),
                tokens,
                adapter_down_weight.reshape(stored * doubled_rank, width),
                adapter_up_weight,
            )
        )
    )
    recv = lax.all_to_all(send, "ad", 0, 0, axis_index_groups=along_z, tiled=True)
    factors = [factors] + [
        lax.ppermute(
            factors, "ad", [(z * N_X + x, z * N_X + (x ^ s)) for z in range(n_z) for x in range(N_X)]
        )
        for s in range(1, N_X)
    ]

    def swap(array, mask):
        return lax.ppermute(array, "tp", [(j, j ^ mask) for j in range(n_tp)])

    def blocks(count, kind):
        return jax.ShapeDtypeStruct((count, tok_rows, columns), kind)

    keep, out = call(base_kernel, (blocks(4, BF16), blocks(4, BF16)), place, tokens, key_value_weight)
    out_recv = swap(out, 1)
    parts, lane_ids = call(
        project,
        (
            jax.ShapeDtypeStruct((n_tp, doubled_rank // 2, rows), BF16),
            jax.ShapeDtypeStruct((8, rows), F32),
        ),
        recv,
        *factors,
        out_recv,
    )
    parts = lax.all_to_all(parts, "tp", 0, 0, tiled=True)
    delta, mark = call(
        apply_up,
        (
            jax.ShapeDtypeStruct((rows, columns), BF16),
            jax.ShapeDtypeStruct((8, LANES), F32),
        ),
        parts,
        lane_ids,
        *factors,
    )
    keep, out = call(halve_kernel, (blocks(2, F32), blocks(2, BF16)), mark, keep, out_recv)
    keep, out = call(halve_kernel, (blocks(1, F32), blocks(1, BF16)), mark, keep, swap(out, 2))
    base_recv = swap(out, 6)
    back = lax.all_to_all(
        delta.reshape(n_z, cap, columns), "ad", 0, 0, axis_index_groups=along_z, tiled=True
    )
    return call(
        mix_kernel,
        jax.ShapeDtypeStruct((tok_rows, columns), BF16),
        place,
        back.reshape(rows, columns),
        keep,
        base_recv,
    )


def solution(mesh):
    return jax.shard_map(
        local,
        mesh=mesh,
        in_specs=(
            P("ad", "tp"),
            P("tp", None),
            P("ad", None, "tp"),
            P("ad", None, "tp"),
            P("ad"),
            P("ad", None),
        ),
        out_specs=P("ad", "tp"),
        check_vma=False,
    )
```

```python
import jax
import jax.numpy as jnp
from jax import lax
from jax.experimental import pallas as pl
from jax.experimental.pallas import tpu as pltpu
from jax.sharding import PartitionSpec as P

ADAPTER_SCALE = 2.0
N_X = 4
MAXLEN = 8
CHAIN = 1

F32 = jnp.float32
BF16 = jnp.bfloat16
NT = (((1,), (1,)), ((), ()))
TN = (((0,), (0,)), ((), ()))
LANES = 128
VMEM_LIMIT = 48 * 1024 * 1024


def iota(shape, dimension):
    return lax.broadcasted_iota(jnp.int32, shape, dimension)


def pack_kernel(
    planes, cap, stored,
    lens_hbm, index_hbm, tokens_hbm, down_hbm, up_hbm,
    send_ref, place_ref, factors_hbm,
    lens_ref, index_ref, tokens_ref, block_ref, up_ref, sems,
):
    requests = lens_ref.shape[1]
    rows, width = tokens_ref.shape
    adapters, rank, columns = up_ref.shape
    down_rows = down_hbm.shape[0]

    def copy(source, target, k):
        made = pltpu.make_async_copy(source, target, sems.at[k])
        made.start()
        return made

    get_lens = copy(lens_hbm, lens_ref, 0)
    get_index = copy(index_hbm, index_ref, 1)
    get_tokens = copy(tokens_hbm, tokens_ref, 2)
    get_down = copy(down_hbm, block_ref.at[pl.ds(0, down_rows)], 3)
    get_up = copy(up_hbm, up_ref, 4)

    get_lens.wait()
    get_index.wait()
    lens = lens_ref[...].astype(F32)
    index = index_ref[...].astype(F32)
    r0, r1 = iota((requests, requests), 0), iota((requests, requests), 1)
    ends = jnp.sum(jnp.where(r1 <= r0, lens, 0.0), axis=1, keepdims=True)
    starts = jnp.sum(jnp.where(r1 < r0, lens, 0.0), axis=1, keepdims=True)
    index_col = jnp.sum(jnp.where(r1 == r0, index, 0.0), axis=1, keepdims=True)
    owner = jnp.floor(index_col * (1.0 / stored))
    same_earlier = (owner == jnp.floor(index * (1.0 / stored))) & (r1 < r0)
    first = jnp.sum(jnp.where(same_earlier, 1.0, 0.0), axis=1, keepdims=True) == 0.0
    within = index_col - owner * stored
    home = jnp.floor(owner * (1.0 / N_X))
    column = owner - home * N_X
    lane = iota((requests, planes), 1).astype(F32)
    counts = jnp.sum(jnp.where(home == lane, 1.0, 0.0), axis=0, keepdims=True)
    number = lane[0:1]
    over = jnp.sum(jnp.where(counts > N_X, number, 0.0), axis=1, keepdims=True)
    under = jnp.sum(jnp.where(counts < N_X, number, 0.0), axis=1, keepdims=True)

    def ahead(steps):
        steps = steps * CHAIN
        return jnp.where(steps < 0.0, steps + planes, steps)

    my_x = lax.axis_index("ad") % N_X
    relative = (column.astype(jnp.int32) ^ my_x).astype(F32)
    in_chain = ahead(home - over) < ahead(under - over)
    handed = in_chain & first & (relative == 0.0)
    target = jnp.where(handed, home + CHAIN, home)
    target = jnp.where(target < 0.0, target + planes, target)
    target = jnp.where(target >= planes, target - planes, target)
    block = jnp.where(handed, float(N_X), relative) * stored + within
    t = iota((requests, rows), 1).astype(F32)
    inside = (t >= starts) & (t < ends)
    plane = jnp.sum(jnp.where(inside, target, 0.0), axis=0, keepdims=True)
    local = jnp.sum(jnp.where(inside, block, 0.0), axis=0, keepdims=True)
    member = iota((planes, rows), 0).astype(F32) == plane
    before = (iota((rows, rows), 0) < iota((rows, rows), 1)).astype(F32).astype(BF16)
    earlier = jnp.dot(member.astype(F32).astype(BF16), before, preferred_element_type=F32)
    rank_in = jnp.sum(jnp.where(member, earlier, 0.0), axis=0, keepdims=True)
    place = (plane * cap + rank_in).astype(jnp.int32)
    place_ref[...] = jnp.broadcast_to(place, place_ref.shape)
    select = (iota((planes * cap, rows), 0) == place).astype(F32).astype(BF16)

    get_up.wait()
    for a in range(adapters):
        pair, side = a // 2, a % 2
        block_ref[
            down_rows + pair * rank : down_rows + (pair + 1) * rank,
            side * columns : (side + 1) * columns,
        ] = up_ref[a]
    get_down.wait()
    put = copy(block_ref, factors_hbm, 5)

    get_tokens.wait()
    packed = jnp.dot(select, tokens_ref[...], preferred_element_type=F32)
    blocks = width // LANES
    for c in range(blocks):
        block = packed[:, c * LANES : (c + 1) * LANES].reshape(planes, cap, LANES)
        send_ref[:, c * cap : (c + 1) * cap, :] = block.astype(BF16)
    at_rank = (iota((LANES, rows), 0).astype(F32) == rank_in).astype(F32).astype(BF16)
    ids = lax.dot_general(
        jnp.where(member, local, 0.0).astype(BF16), at_rank, NT, preferred_element_type=F32
    )
    ids = jnp.broadcast_to(ids.reshape(planes, 1, LANES), (planes, 8, LANES))
    send_ref[:, blocks * cap :, :] = ids.astype(BF16)
    put.wait()


def base_kernel(place_ref, tokens_ref, weight_ref, keep_ref, send_ref):
    del place_ref
    columns = keep_ref.shape[2]
    me = lax.axis_index("tp")

    def block(relative):
        first = pl.multiple_of((me ^ relative) * columns, columns)
        return jnp.dot(
            tokens_ref[...], weight_ref[:, pl.ds(first, columns)], preferred_element_type=F32
        ).astype(BF16)

    for k, relative in enumerate((0, 6, 2, 4)):
        send_ref[k] = block(relative ^ 1)
        keep_ref[k] = block(relative)


def halve_kernel(after_ref, keep_ref, recv_ref, kept_ref, send_ref):
    del after_ref
    half = kept_ref.shape[0]
    for k in range(half):
        kept_ref[k] = keep_ref[k].astype(F32) + recv_ref[k].astype(F32)
        send_ref[k] = (keep_ref[half + k].astype(F32) + recv_ref[half + k].astype(F32)).astype(BF16)


def low_kernel(
    planes, cap, stored, recv_ref, f0_ref, f1_ref, f2_ref, f3_ref,
    handed_ref, kept_ref, out_ref, lane_ids_ref
):
    del kept_ref
    rows = planes * cap
    blocks = recv_ref.shape[1] // cap
    source = iota((planes, rows), 0)
    p = iota((planes, rows), 1)
    mine = (p >= source * cap) & (p < source * cap + cap)
    offset = jnp.sum(jnp.where(mine, p - source * cap, 0).astype(F32), axis=0, keepdims=True)
    spread = (iota((LANES, rows), 0).astype(F32) == offset).astype(F32).astype(BF16)
    ids = recv_ref[:, blocks * cap :, :].astype(F32)[:, 0, :].astype(BF16)
    ids = jnp.dot(ids, spread, preferred_element_type=F32)
    ids = jnp.sum(jnp.where(mine, ids, 0.0), axis=0, keepdims=True)
    lane_ids_ref[...] = jnp.broadcast_to(ids, lane_ids_ref.shape)
    recv = jnp.concatenate(
        [
            recv_ref[:, c * cap : (c + 1) * cap, :].astype(F32).reshape(rows, LANES).astype(BF16)
            for c in range(blocks)
        ],
        axis=1,
    )
    n, rank = out_ref.shape[:2]
    doubled = 2 * rank
    low = jnp.zeros((doubled, rows), F32)
    for x, factors_ref in enumerate((f0_ref, f1_ref, f2_ref, f3_ref, handed_ref)):
        block = factors_ref[: stored * doubled, :]
        values = lax.dot_general(block, recv, NT, preferred_element_type=F32)
        for a in range(stored):
            low = jnp.where(
                ids == float(x * stored + a), values[a * doubled : (a + 1) * doubled], low
            )
    low = low.astype(BF16)
    for j in range(n):
        half = j * 2 // n
        out_ref[j] = low[half * rank : (half + 1) * rank]


def delta_kernel(
    stored, parts_ref, lane_ids_ref, f0_ref, f1_ref, f2_ref, f3_ref,
    handed_ref, out_ref, mark_ref
):
    low = parts_ref[0].astype(F32)
    for j in range(1, parts_ref.shape[0]):
        low = low + parts_ref[j].astype(F32)
    rank = low.shape[0]
    columns = out_ref.shape[1]
    ids = lane_ids_ref[0:1, :]
    spread, up = [], []
    for x, factors_ref in enumerate((f0_ref, f1_ref, f2_ref, f3_ref, handed_ref)):
        for side in range(2):
            up.append(factors_ref[stored * 2 * rank :, side * columns : (side + 1) * columns])
            for pair in range(stored // 2):
                a = float(x * stored + 2 * pair + side)
                spread.append(jnp.where(ids == a, low, 0.0).astype(BF16))
    product = lax.dot_general(
        jnp.concatenate(spread, axis=0), jnp.concatenate(up, axis=0), TN, preferred_element_type=F32
    )
    out_ref[...] = product.astype(BF16)
    mark_ref[...] = jnp.zeros(mark_ref.shape, F32)


def mix_kernel(place_ref, back_ref, kept_ref, recv_ref, out_ref):
    rows = out_ref.shape[0]
    place = place_ref[0:1, :]
    select = (iota((back_ref.shape[0], rows), 0) == place).astype(F32).astype(BF16)
    delta = lax.dot_general(select, back_ref[...], TN, preferred_element_type=F32)
    base = kept_ref[0] + recv_ref[0].astype(F32)
    out_ref[...] = (base + ADAPTER_SCALE * delta).astype(BF16)


def call(kernel, out_shape, *args, cost=None):
    return pl.pallas_call(
        kernel,
        out_shape=out_shape,
        compiler_params=pltpu.CompilerParams(vmem_limit_bytes=VMEM_LIMIT),
        cost_estimate=cost,
    )(*args)


def in_hbm(array):
    return pltpu.with_memory_space_constraint(array, pltpu.HBM)


def local(
    tokens, key_value_weight, adapter_down_weight, adapter_up_weight, request_adapter_index, lengths
):
    tok_rows, width = tokens.shape
    n_ad = lax.axis_size("ad")
    n_tp = lax.axis_size("tp")
    n_z = n_ad // N_X
    stored, doubled_rank, _ = adapter_down_weight.shape
    rank, columns = adapter_up_weight.shape[1:]
    cap = N_X * MAXLEN
    rows = n_z * cap
    along_x = [[z * N_X + x for x in range(N_X)] for z in range(n_z)]
    along_z = [[z * N_X + x for z in range(n_z)] for x in range(N_X)]

    def pack(*refs):
        pack_kernel(n_z, cap, stored, *refs)

    def project(*refs):
        low_kernel(n_z, cap, stored, *refs)

    def apply_up(*refs):
        delta_kernel(stored, *refs)

    hbm = pl.BlockSpec(memory_space=pltpu.HBM)
    vmem = pl.BlockSpec(memory_space=pltpu.VMEM)
    block_rows = stored * doubled_rank + stored // 2 * rank
    send, place, factors = pl.pallas_call(
        pack,
        out_shape=(
            jax.ShapeDtypeStruct((n_z, width // LANES * cap + 8, LANES), BF16),
            jax.ShapeDtypeStruct((8, tok_rows), jnp.int32),
            jax.ShapeDtypeStruct((block_rows, width), BF16),
        ),
        in_specs=[hbm] * 5,
        out_specs=(vmem, vmem, hbm),
        scratch_shapes=[
            pltpu.VMEM((1, lengths.shape[1]), jnp.int32),
            pltpu.VMEM((1, lengths.shape[1]), jnp.int32),
            pltpu.VMEM((tok_rows, width), BF16),
            pltpu.VMEM((block_rows, width), BF16),
            pltpu.VMEM((stored, rank, columns), BF16),
            pltpu.SemaphoreType.DMA((6,)),
        ],
        compiler_params=pltpu.CompilerParams(vmem_limit_bytes=VMEM_LIMIT),
    )(
        *(
            pltpu.with_memory_space_constraint(array, pltpu.HBM)
            for array in (
                lengths,
                request_adapter_index.reshape(1, -1),
                tokens,
                adapter_down_weight.reshape(stored * doubled_rank, width),
                adapter_up_weight,
            )
        )
    )
    recv = lax.all_to_all(send, "ad", 0, 0, axis_index_groups=along_z, tiled=True)
    factors = [factors] + [
        lax.ppermute(
            factors, "ad", [(z * N_X + x, z * N_X + (x ^ s)) for z in range(n_z) for x in range(N_X)]
        )
        for s in range(1, N_X)
    ]

    handed = lax.ppermute(
        factors[0],
        "ad",
        [(z * N_X + x, (z + CHAIN) % n_z * N_X + x) for z in range(n_z) for x in range(N_X)],
    )

    def swap(array, mask):
        return lax.ppermute(array, "tp", [(j, j ^ mask) for j in range(n_tp)])

    def blocks(count, kind):
        return jax.ShapeDtypeStruct((count, tok_rows, columns), kind)

    much = pl.CostEstimate(flops=4 * 10**10, bytes_accessed=tokens.size, transcendentals=0)
    keep, out = call(base_kernel, (blocks(4, BF16), blocks(4, BF16)), handed, in_hbm(tokens), in_hbm(key_value_weight), cost=much)
    out_recv = swap(out, 1)
    parts, lane_ids = call(
        project,
        (
            jax.ShapeDtypeStruct((n_tp, doubled_rank // 2, rows), BF16),
            jax.ShapeDtypeStruct((8, rows), F32),
        ),
        recv,
        *factors,
        handed,
        out_recv,
    )
    parts = lax.all_to_all(parts, "tp", 0, 0, tiled=True)
    delta, mark = call(
        apply_up,
        (
            jax.ShapeDtypeStruct((rows, columns), BF16),
            jax.ShapeDtypeStruct((8, LANES), F32),
        ),
        parts,
        lane_ids,
        *factors,
        handed,
    )
    keep, out = call(halve_kernel, (blocks(2, F32), blocks(2, BF16)), mark, keep, out_recv)
    keep, out = call(halve_kernel, (blocks(1, F32), blocks(1, BF16)), mark, keep, swap(out, 2))
    base_recv = swap(out, 6)
    back = lax.all_to_all(
        delta.reshape(n_z, cap, columns), "ad", 0, 0, axis_index_groups=along_z, tiled=True
    )
    return call(
        mix_kernel,
        jax.ShapeDtypeStruct((tok_rows, columns), BF16),
        place,
        back.reshape(rows, columns),
        keep,
        base_recv,
    )


def solution(mesh):
    return jax.shard_map(
        local,
        mesh=mesh,
        in_specs=(
            P("ad", "tp"),
            P("tp", None),
            P("ad", None, "tp"),
            P("ad", None, "tp"),
            P("ad"),
            P("ad", None),
        ),
        out_specs=P("ad", "tp"),
        check_vma=False,
    )
```

```python
import jax
import jax.numpy as jnp
from jax import lax
from jax.experimental import pallas as pl
from jax.experimental.pallas import tpu as pltpu
from jax.sharding import PartitionSpec as P

ADAPTER_SCALE = 2.0
N_X = 4
MAXLEN = 8
CHAIN = 1

F32 = jnp.float32
BF16 = jnp.bfloat16
NT = (((1,), (1,)), ((), ()))
TN = (((0,), (0,)), ((), ()))
LANES = 128
VMEM_LIMIT = 48 * 1024 * 1024


def iota(shape, dimension):
    return lax.broadcasted_iota(jnp.int32, shape, dimension)


def pack_kernel(
    planes, cap, stored,
    lens_hbm, index_hbm, tokens_hbm, down_hbm, up_hbm,
    send_ref, place_ref, factors_hbm,
    lens_ref, index_ref, tokens_ref, block_ref, up_ref, sems,
):
    requests = lens_ref.shape[1]
    rows, width = tokens_ref.shape
    adapters, rank, columns = up_ref.shape
    down_rows = down_hbm.shape[0]

    def copy(source, target, k):
        made = pltpu.make_async_copy(source, target, sems.at[k])
        made.start()
        return made

    get_lens = copy(lens_hbm, lens_ref, 0)
    get_index = copy(index_hbm, index_ref, 1)
    get_tokens = copy(tokens_hbm, tokens_ref, 2)
    get_down = copy(down_hbm, block_ref.at[pl.ds(0, down_rows)], 3)
    get_up = copy(up_hbm, up_ref, 4)

    get_lens.wait()
    get_index.wait()
    lens = lens_ref[...].astype(F32)
    index = index_ref[...].astype(F32)
    r0, r1 = iota((requests, requests), 0), iota((requests, requests), 1)
    ends = jnp.sum(jnp.where(r1 <= r0, lens, 0.0), axis=1, keepdims=True)
    starts = jnp.sum(jnp.where(r1 < r0, lens, 0.0), axis=1, keepdims=True)
    index_col = jnp.sum(jnp.where(r1 == r0, index, 0.0), axis=1, keepdims=True)
    owner = jnp.floor(index_col * (1.0 / stored))
    same_earlier = (owner == jnp.floor(index * (1.0 / stored))) & (r1 < r0)
    first = jnp.sum(jnp.where(same_earlier, 1.0, 0.0), axis=1, keepdims=True) == 0.0
    within = index_col - owner * stored
    home = jnp.floor(owner * (1.0 / N_X))
    column = owner - home * N_X
    lane = iota((requests, planes), 1).astype(F32)
    counts = jnp.sum(jnp.where(home == lane, 1.0, 0.0), axis=0, keepdims=True)
    number = lane[0:1]
    over = jnp.sum(jnp.where(counts > N_X, number, 0.0), axis=1, keepdims=True)
    under = jnp.sum(jnp.where(counts < N_X, number, 0.0), axis=1, keepdims=True)

    def ahead(steps):
        steps = steps * CHAIN
        return jnp.where(steps < 0.0, steps + planes, steps)

    my_x = lax.axis_index("ad") % N_X
    relative = (column.astype(jnp.int32) ^ my_x).astype(F32)
    in_chain = ahead(home - over) < ahead(under - over)
    handed = in_chain & first & (relative == 0.0)
    target = jnp.where(handed, home + CHAIN, home)
    target = jnp.where(target < 0.0, target + planes, target)
    target = jnp.where(target >= planes, target - planes, target)
    block = jnp.where(handed, float(N_X), relative) * stored + within
    t = iota((requests, rows), 1).astype(F32)
    inside = (t >= starts) & (t < ends)
    plane = jnp.sum(jnp.where(inside, target, 0.0), axis=0, keepdims=True)
    local = jnp.sum(jnp.where(inside, block, 0.0), axis=0, keepdims=True)
    member = iota((planes, rows), 0).astype(F32) == plane
    before = (iota((rows, rows), 0) < iota((rows, rows), 1)).astype(F32).astype(BF16)
    earlier = jnp.dot(member.astype(F32).astype(BF16), before, preferred_element_type=F32)
    rank_in = jnp.sum(jnp.where(member, earlier, 0.0), axis=0, keepdims=True)
    place = (plane * cap + rank_in).astype(jnp.int32)
    place_ref[...] = jnp.broadcast_to(place, place_ref.shape)
    select = (iota((planes * cap, rows), 0) == place).astype(F32).astype(BF16)

    get_up.wait()
    for a in range(adapters):
        pair, side = a // 2, a % 2
        block_ref[
            down_rows + pair * rank : down_rows + (pair + 1) * rank,
            side * columns : (side + 1) * columns,
        ] = up_ref[a]
    get_down.wait()
    put = copy(block_ref, factors_hbm, 5)

    get_tokens.wait()
    packed = jnp.dot(select, tokens_ref[...], preferred_element_type=F32)
    blocks = width // LANES
    for c in range(blocks):
        block = packed[:, c * LANES : (c + 1) * LANES].reshape(planes, cap, LANES)
        send_ref[:, c * cap : (c + 1) * cap, :] = block.astype(BF16)
    at_rank = (iota((LANES, rows), 0).astype(F32) == rank_in).astype(F32).astype(BF16)
    ids = lax.dot_general(
        jnp.where(member, local, 0.0).astype(BF16), at_rank, NT, preferred_element_type=F32
    )
    ids = jnp.broadcast_to(ids.reshape(planes, 1, LANES), (planes, 8, LANES))
    send_ref[:, blocks * cap :, :] = ids.astype(BF16)
    put.wait()


def base_kernel(place_ref, tokens_ref, weight_ref, keep_ref, send_ref):
    del place_ref
    columns = keep_ref.shape[2]
    me = lax.axis_index("tp")

    def block(relative):
        first = pl.multiple_of((me ^ relative) * columns, columns)
        return jnp.dot(
            tokens_ref[...], weight_ref[:, pl.ds(first, columns)], preferred_element_type=F32
        ).astype(BF16)

    for k, relative in enumerate((0, 6, 2, 4)):
        send_ref[k] = block(relative ^ 1)
        keep_ref[k] = block(relative)


def pair_kernel(after_ref, keep_ref, recv_ref, kept_ref, *send_refs):
    del after_ref
    kept_ref[0] = keep_ref[0].astype(F32) + recv_ref[0].astype(F32)
    for k, send_ref in enumerate(send_refs, 1):
        send_ref[0] = (keep_ref[k].astype(F32) + recv_ref[k].astype(F32)).astype(BF16)


def low_kernel(
    planes, cap, stored, recv_ref, f0_ref, f1_ref, f2_ref, f3_ref,
    handed_ref, kept_ref, out_ref, lane_ids_ref
):
    del kept_ref
    rows = planes * cap
    blocks = recv_ref.shape[1] // cap
    source = iota((planes, rows), 0)
    p = iota((planes, rows), 1)
    mine = (p >= source * cap) & (p < source * cap + cap)
    offset = jnp.sum(jnp.where(mine, p - source * cap, 0).astype(F32), axis=0, keepdims=True)
    spread = (iota((LANES, rows), 0).astype(F32) == offset).astype(F32).astype(BF16)
    ids = recv_ref[:, blocks * cap :, :].astype(F32)[:, 0, :].astype(BF16)
    ids = jnp.dot(ids, spread, preferred_element_type=F32)
    ids = jnp.sum(jnp.where(mine, ids, 0.0), axis=0, keepdims=True)
    lane_ids_ref[...] = jnp.broadcast_to(ids, lane_ids_ref.shape)
    recv = jnp.concatenate(
        [
            recv_ref[:, c * cap : (c + 1) * cap, :].astype(F32).reshape(rows, LANES).astype(BF16)
            for c in range(blocks)
        ],
        axis=1,
    )
    n, rank = out_ref.shape[:2]
    doubled = 2 * rank
    low = jnp.zeros((doubled, rows), F32)
    for x, factors_ref in enumerate((f0_ref, f1_ref, f2_ref, f3_ref, handed_ref)):
        block = factors_ref[: stored * doubled, :]
        values = lax.dot_general(block, recv, NT, preferred_element_type=F32)
        for a in range(stored):
            low = jnp.where(
                ids == float(x * stored + a), values[a * doubled : (a + 1) * doubled], low
            )
    low = low.astype(BF16)
    for j in range(n):
        half = j * 2 // n
        out_ref[j] = low[half * rank : (half + 1) * rank]


def delta_kernel(
    stored, parts_ref, lane_ids_ref, f0_ref, f1_ref, f2_ref, f3_ref,
    handed_ref, out_ref, mark_ref
):
    low = parts_ref[0].astype(F32)
    for j in range(1, parts_ref.shape[0]):
        low = low + parts_ref[j].astype(F32)
    rank = low.shape[0]
    columns = out_ref.shape[1]
    ids = lane_ids_ref[0:1, :]
    spread, up = [], []
    for x, factors_ref in enumerate((f0_ref, f1_ref, f2_ref, f3_ref, handed_ref)):
        for side in range(2):
            up.append(factors_ref[stored * 2 * rank :, side * columns : (side + 1) * columns])
            for pair in range(stored // 2):
                a = float(x * stored + 2 * pair + side)
                spread.append(jnp.where(ids == a, low, 0.0).astype(BF16))
    product = lax.dot_general(
        jnp.concatenate(spread, axis=0), jnp.concatenate(up, axis=0), TN, preferred_element_type=F32
    )
    out_ref[...] = product.astype(BF16)
    mark_ref[...] = jnp.zeros(mark_ref.shape, F32)


def mix_kernel(place_ref, back_ref, kept_ref, r0_ref, r1_ref, r2_ref, out_ref):
    rows = out_ref.shape[0]
    place = place_ref[0:1, :]
    select = (iota((back_ref.shape[0], rows), 0) == place).astype(F32).astype(BF16)
    delta = lax.dot_general(select, back_ref[...], TN, preferred_element_type=F32)
    base = kept_ref[0]
    for recv_ref in (r0_ref, r1_ref, r2_ref):
        base = base + recv_ref[0].astype(F32)
    out_ref[...] = (base + ADAPTER_SCALE * delta).astype(BF16)


def call(kernel, out_shape, *args, cost=None):
    return pl.pallas_call(
        kernel,
        out_shape=out_shape,
        compiler_params=pltpu.CompilerParams(vmem_limit_bytes=VMEM_LIMIT),
        cost_estimate=cost,
    )(*args)


def in_hbm(array):
    return pltpu.with_memory_space_constraint(array, pltpu.HBM)


def local(
    tokens, key_value_weight, adapter_down_weight, adapter_up_weight, request_adapter_index, lengths
):
    tok_rows, width = tokens.shape
    n_ad = lax.axis_size("ad")
    n_tp = lax.axis_size("tp")
    n_z = n_ad // N_X
    stored, doubled_rank, _ = adapter_down_weight.shape
    rank, columns = adapter_up_weight.shape[1:]
    cap = N_X * MAXLEN
    rows = n_z * cap
    along_x = [[z * N_X + x for x in range(N_X)] for z in range(n_z)]
    along_z = [[z * N_X + x for z in range(n_z)] for x in range(N_X)]

    def pack(*refs):
        pack_kernel(n_z, cap, stored, *refs)

    def project(*refs):
        low_kernel(n_z, cap, stored, *refs)

    def apply_up(*refs):
        delta_kernel(stored, *refs)

    hbm = pl.BlockSpec(memory_space=pltpu.HBM)
    vmem = pl.BlockSpec(memory_space=pltpu.VMEM)
    block_rows = stored * doubled_rank + stored // 2 * rank
    send, place, factors = pl.pallas_call(
        pack,
        out_shape=(
            jax.ShapeDtypeStruct((n_z, width // LANES * cap + 8, LANES), BF16),
            jax.ShapeDtypeStruct((8, tok_rows), jnp.int32),
            jax.ShapeDtypeStruct((block_rows, width), BF16),
        ),
        in_specs=[hbm] * 5,
        out_specs=(vmem, vmem, hbm),
        scratch_shapes=[
            pltpu.VMEM((1, lengths.shape[1]), jnp.int32),
            pltpu.VMEM((1, lengths.shape[1]), jnp.int32),
            pltpu.VMEM((tok_rows, width), BF16),
            pltpu.VMEM((block_rows, width), BF16),
            pltpu.VMEM((stored, rank, columns), BF16),
            pltpu.SemaphoreType.DMA((6,)),
        ],
        compiler_params=pltpu.CompilerParams(vmem_limit_bytes=VMEM_LIMIT),
    )(
        *(
            pltpu.with_memory_space_constraint(array, pltpu.HBM)
            for array in (
                lengths,
                request_adapter_index.reshape(1, -1),
                tokens,
                adapter_down_weight.reshape(stored * doubled_rank, width),
                adapter_up_weight,
            )
        )
    )
    recv = lax.all_to_all(send, "ad", 0, 0, axis_index_groups=along_z, tiled=True)
    factors = [factors] + [
        lax.ppermute(
            factors, "ad", [(z * N_X + x, z * N_X + (x ^ s)) for z in range(n_z) for x in range(N_X)]
        )
        for s in range(1, N_X)
    ]

    handed = lax.ppermute(
        factors[0],
        "ad",
        [(z * N_X + x, (z + CHAIN) % n_z * N_X + x) for z in range(n_z) for x in range(N_X)],
    )

    def swap(array, mask):
        return lax.ppermute(array, "tp", [(j, j ^ mask) for j in range(n_tp)])

    def blocks(count, kind):
        return jax.ShapeDtypeStruct((count, tok_rows, columns), kind)

    much = pl.CostEstimate(flops=4 * 10**10, bytes_accessed=tokens.size, transcendentals=0)
    keep, out = call(base_kernel, (blocks(4, BF16), blocks(4, BF16)), handed, in_hbm(tokens), in_hbm(key_value_weight), cost=much)
    out_recv = swap(out, 1)
    parts, lane_ids = call(
        project,
        (
            jax.ShapeDtypeStruct((n_tp, doubled_rank // 2, rows), BF16),
            jax.ShapeDtypeStruct((8, rows), F32),
        ),
        recv,
        *factors,
        handed,
        out_recv,
    )
    parts = lax.all_to_all(parts, "tp", 0, 0, tiled=True)
    delta, mark = call(
        apply_up,
        (
            jax.ShapeDtypeStruct((rows, columns), BF16),
            jax.ShapeDtypeStruct((8, LANES), F32),
        ),
        parts,
        lane_ids,
        *factors,
        handed,
    )
    shares = call(pair_kernel, (blocks(1, F32),) + (blocks(1, BF16),) * 3, mark, keep, out_recv)
    shares = shares[:1] + tuple(
        swap(share, mask) for share, mask in zip(shares[1:], (6, 2, 4), strict=True)
    )
    back = lax.all_to_all(
        delta.reshape(n_z, cap, columns), "ad", 0, 0, axis_index_groups=along_z, tiled=True
    )
    return call(
        mix_kernel,
        jax.ShapeDtypeStruct((tok_rows, columns), BF16),
        place,
        back.reshape(rows, columns),
        *shares,
    )


def solution(mesh):
    return jax.shard_map(
        local,
        mesh=mesh,
        in_specs=(
            P("ad", "tp"),
            P("tp", None),
            P("ad", None, "tp"),
            P("ad", None, "tp"),
            P("ad"),
            P("ad", None),
        ),
        out_specs=P("ad", "tp"),
        check_vma=False,
    )
```

```python
import jax
import jax.numpy as jnp
from jax import lax
from jax.experimental import pallas as pl
from jax.experimental.pallas import tpu as pltpu
from jax.sharding import PartitionSpec as P

ADAPTER_SCALE = 2.0
N_X = 4
MAXLEN = 8
CHAIN = 1

F32 = jnp.float32
BF16 = jnp.bfloat16
NT = (((1,), (1,)), ((), ()))
TN = (((0,), (0,)), ((), ()))
LANES = 128
VMEM_LIMIT = 48 * 1024 * 1024


def iota(shape, dimension):
    return lax.broadcasted_iota(jnp.int32, shape, dimension)


def pack_kernel(
    planes, cap, stored,
    lens_hbm, index_hbm, tokens_hbm, down_hbm, up_hbm,
    send_ref, place_ref, factors_hbm,
    lens_ref, index_ref, tokens_ref, block_ref, up_ref, sems,
):
    requests = lens_ref.shape[1]
    rows, width = tokens_ref.shape
    adapters, rank, columns = up_ref.shape
    down_rows = down_hbm.shape[0]

    def copy(source, target, k):
        made = pltpu.make_async_copy(source, target, sems.at[k])
        made.start()
        return made

    get_lens = copy(lens_hbm, lens_ref, 0)
    get_index = copy(index_hbm, index_ref, 1)
    get_tokens = copy(tokens_hbm, tokens_ref, 2)
    get_down = copy(down_hbm, block_ref.at[pl.ds(0, down_rows)], 3)
    get_up = copy(up_hbm, up_ref, 4)

    get_lens.wait()
    get_index.wait()
    lens = lens_ref[...].astype(F32)
    index = index_ref[...].astype(F32)
    r0, r1 = iota((requests, requests), 0), iota((requests, requests), 1)
    ends = jnp.sum(jnp.where(r1 <= r0, lens, 0.0), axis=1, keepdims=True)
    starts = jnp.sum(jnp.where(r1 < r0, lens, 0.0), axis=1, keepdims=True)
    index_col = jnp.sum(jnp.where(r1 == r0, index, 0.0), axis=1, keepdims=True)
    owner = jnp.floor(index_col * (1.0 / stored))
    same_earlier = (owner == jnp.floor(index * (1.0 / stored))) & (r1 < r0)
    first = jnp.sum(jnp.where(same_earlier, 1.0, 0.0), axis=1, keepdims=True) == 0.0
    within = index_col - owner * stored
    home = jnp.floor(owner * (1.0 / N_X))
    column = owner - home * N_X
    lane = iota((requests, planes), 1).astype(F32)
    counts = jnp.sum(jnp.where(home == lane, 1.0, 0.0), axis=0, keepdims=True)
    number = lane[0:1]
    over = jnp.sum(jnp.where(counts > N_X, number, 0.0), axis=1, keepdims=True)
    under = jnp.sum(jnp.where(counts < N_X, number, 0.0), axis=1, keepdims=True)

    def ahead(steps):
        steps = steps * CHAIN
        return jnp.where(steps < 0.0, steps + planes, steps)

    my_x = lax.axis_index("ad") % N_X
    relative = (column.astype(jnp.int32) ^ my_x).astype(F32)
    in_chain = ahead(home - over) < ahead(under - over)
    handed = in_chain & first & (relative == 0.0)
    target = jnp.where(handed, home + CHAIN, home)
    target = jnp.where(target < 0.0, target + planes, target)
    target = jnp.where(target >= planes, target - planes, target)
    block = jnp.where(handed, float(N_X), relative) * stored + within
    t = iota((requests, rows), 1).astype(F32)
    inside = (t >= starts) & (t < ends)
    plane = jnp.sum(jnp.where(inside, target, 0.0), axis=0, keepdims=True)
    local = jnp.sum(jnp.where(inside, block, 0.0), axis=0, keepdims=True)
    member = iota((planes, rows), 0).astype(F32) == plane
    before = (iota((rows, rows), 0) < iota((rows, rows), 1)).astype(F32).astype(BF16)
    earlier = jnp.dot(member.astype(F32).astype(BF16), before, preferred_element_type=F32)
    rank_in = jnp.sum(jnp.where(member, earlier, 0.0), axis=0, keepdims=True)
    place = (plane * cap + rank_in).astype(jnp.int32)
    place_ref[...] = jnp.broadcast_to(place, place_ref.shape)
    select = (iota((planes * cap, rows), 0) == place).astype(F32).astype(BF16)

    get_up.wait()
    for a in range(adapters):
        pair, side = a // 2, a % 2
        block_ref[
            down_rows + pair * rank : down_rows + (pair + 1) * rank,
            side * columns : (side + 1) * columns,
        ] = up_ref[a]
    get_down.wait()
    put = copy(block_ref, factors_hbm, 5)

    get_tokens.wait()
    packed = jnp.dot(select, tokens_ref[...], preferred_element_type=F32)
    blocks = width // LANES
    for c in range(blocks):
        block = packed[:, c * LANES : (c + 1) * LANES].reshape(planes, cap, LANES)
        send_ref[:, c * cap : (c + 1) * cap, :] = block.astype(BF16)
    at_rank = (iota((LANES, rows), 0).astype(F32) == rank_in).astype(F32).astype(BF16)
    ids = lax.dot_general(
        jnp.where(member, local, 0.0).astype(BF16), at_rank, NT, preferred_element_type=F32
    )
    ids = jnp.broadcast_to(ids.reshape(planes, 1, LANES), (planes, 8, LANES))
    send_ref[:, blocks * cap :, :] = ids.astype(BF16)
    put.wait()


def base_kernel(place_ref, tokens_ref, weight_ref, keep_ref, send_ref):
    del place_ref
    columns = keep_ref.shape[2]
    me = lax.axis_index("tp")

    def block(relative):
        first = pl.multiple_of((me ^ relative) * columns, columns)
        return jnp.dot(
            tokens_ref[...], weight_ref[:, pl.ds(first, columns)], preferred_element_type=F32
        ).astype(BF16)

    for k, relative in enumerate((0, 6, 2, 4)):
        send_ref[k] = block(relative ^ 1)
        keep_ref[k] = block(relative)


def pair_kernel(after_ref, keep_ref, recv_ref, kept_ref, *send_refs):
    del after_ref
    kept_ref[0] = keep_ref[0].astype(F32) + recv_ref[0].astype(F32)
    for k, send_ref in enumerate(send_refs, 1):
        send_ref[0] = (keep_ref[k].astype(F32) + recv_ref[k].astype(F32)).astype(BF16)


def low_kernel(
    planes, cap, stored, recv_ref, f0_ref, f1_ref, f2_ref, f3_ref,
    handed_ref, kept_ref, out_ref, lane_ids_ref
):
    del kept_ref
    rows = planes * cap
    blocks = recv_ref.shape[1] // cap
    source = iota((planes, rows), 0)
    p = iota((planes, rows), 1)
    mine = (p >= source * cap) & (p < source * cap + cap)
    offset = jnp.sum(jnp.where(mine, p - source * cap, 0).astype(F32), axis=0, keepdims=True)
    spread = (iota((LANES, rows), 0).astype(F32) == offset).astype(F32).astype(BF16)
    ids = recv_ref[:, blocks * cap :, :].astype(F32)[:, 0, :].astype(BF16)
    ids = jnp.dot(ids, spread, preferred_element_type=F32)
    ids = jnp.sum(jnp.where(mine, ids, 0.0), axis=0, keepdims=True)
    lane_ids_ref[...] = jnp.broadcast_to(ids, lane_ids_ref.shape)
    recv = jnp.concatenate(
        [
            recv_ref[:, c * cap : (c + 1) * cap, :].astype(F32).reshape(rows, LANES).astype(BF16)
            for c in range(blocks)
        ],
        axis=1,
    )
    n, rank = out_ref.shape[:2]
    doubled = 2 * rank
    low = jnp.zeros((doubled, rows), F32)
    for x, factors_ref in enumerate((f0_ref, f1_ref, f2_ref, f3_ref, handed_ref)):
        block = factors_ref[: stored * doubled, :]
        values = lax.dot_general(block, recv, NT, preferred_element_type=F32)
        for a in range(stored):
            low = jnp.where(
                ids == float(x * stored + a), values[a * doubled : (a + 1) * doubled], low
            )
    low = low.astype(BF16)
    for j in range(n):
        half = j * 2 // n
        out_ref[j] = low[half * rank : (half + 1) * rank]


def delta_kernel(
    stored, parts_ref, lane_ids_ref, f0_ref, f1_ref, f2_ref, f3_ref,
    handed_ref, out_ref, mark_ref
):
    low = parts_ref[0].astype(F32)
    for j in range(1, parts_ref.shape[0]):
        low = low + parts_ref[j].astype(F32)
    rank = low.shape[0]
    columns = out_ref.shape[1]
    ids = lane_ids_ref[0:1, :]
    spread, up = [], []
    for x, factors_ref in enumerate((f0_ref, f1_ref, f2_ref, f3_ref, handed_ref)):
        for side in range(2):
            up.append(factors_ref[stored * 2 * rank :, side * columns : (side + 1) * columns])
            for pair in range(stored // 2):
                a = float(x * stored + 2 * pair + side)
                spread.append(jnp.where(ids == a, low, 0.0).astype(BF16))
    product = lax.dot_general(
        jnp.concatenate(spread, axis=0), jnp.concatenate(up, axis=0), TN, preferred_element_type=F32
    )
    out_ref[...] = product.astype(BF16)
    mark_ref[...] = jnp.zeros(mark_ref.shape, F32)


def ready_kernel(place_ref, kept_ref, r0_ref, r1_ref, r2_ref, base_ref, select_ref):
    base = kept_ref[0]
    for recv_ref in (r0_ref, r1_ref, r2_ref):
        base = base + recv_ref[0].astype(F32)
    base_ref[...] = base
    places, rows = select_ref.shape[1], select_ref.shape[0]
    select = (iota((places, rows), 0) == place_ref[0:1, :]).astype(F32)
    select_ref[...] = select.T.astype(BF16)


def mix_kernel(back_ref, base_ref, select_ref, out_ref):
    delta = jnp.dot(select_ref[...], back_ref[...], preferred_element_type=F32)
    out_ref[...] = (base_ref[...] + ADAPTER_SCALE * delta).astype(BF16)


def call(kernel, out_shape, *args, cost=None):
    return pl.pallas_call(
        kernel,
        out_shape=out_shape,
        compiler_params=pltpu.CompilerParams(vmem_limit_bytes=VMEM_LIMIT),
        cost_estimate=cost,
    )(*args)


def in_hbm(array):
    return pltpu.with_memory_space_constraint(array, pltpu.HBM)


def local(
    tokens, key_value_weight, adapter_down_weight, adapter_up_weight, request_adapter_index, lengths
):
    tok_rows, width = tokens.shape
    n_ad = lax.axis_size("ad")
    n_tp = lax.axis_size("tp")
    n_z = n_ad // N_X
    stored, doubled_rank, _ = adapter_down_weight.shape
    rank, columns = adapter_up_weight.shape[1:]
    cap = N_X * MAXLEN
    rows = n_z * cap
    along_x = [[z * N_X + x for x in range(N_X)] for z in range(n_z)]
    along_z = [[z * N_X + x for z in range(n_z)] for x in range(N_X)]

    def pack(*refs):
        pack_kernel(n_z, cap, stored, *refs)

    def project(*refs):
        low_kernel(n_z, cap, stored, *refs)

    def apply_up(*refs):
        delta_kernel(stored, *refs)

    hbm = pl.BlockSpec(memory_space=pltpu.HBM)
    vmem = pl.BlockSpec(memory_space=pltpu.VMEM)
    block_rows = stored * doubled_rank + stored // 2 * rank
    send, place, factors = pl.pallas_call(
        pack,
        out_shape=(
            jax.ShapeDtypeStruct((n_z, width // LANES * cap + 8, LANES), BF16),
            jax.ShapeDtypeStruct((8, tok_rows), jnp.int32),
            jax.ShapeDtypeStruct((block_rows, width), BF16),
        ),
        in_specs=[hbm] * 5,
        out_specs=(vmem, vmem, hbm),
        scratch_shapes=[
            pltpu.VMEM((1, lengths.shape[1]), jnp.int32),
            pltpu.VMEM((1, lengths.shape[1]), jnp.int32),
            pltpu.VMEM((tok_rows, width), BF16),
            pltpu.VMEM((block_rows, width), BF16),
            pltpu.VMEM((stored, rank, columns), BF16),
            pltpu.SemaphoreType.DMA((6,)),
        ],
        compiler_params=pltpu.CompilerParams(vmem_limit_bytes=VMEM_LIMIT),
    )(
        *(
            pltpu.with_memory_space_constraint(array, pltpu.HBM)
            for array in (
                lengths,
                request_adapter_index.reshape(1, -1),
                tokens,
                adapter_down_weight.reshape(stored * doubled_rank, width),
                adapter_up_weight,
            )
        )
    )
    recv = lax.all_to_all(send, "ad", 0, 0, axis_index_groups=along_z, tiled=True)
    factors = [factors] + [
        lax.ppermute(
            factors, "ad", [(z * N_X + x, z * N_X + (x ^ s)) for z in range(n_z) for x in range(N_X)]
        )
        for s in range(1, N_X)
    ]

    handed = lax.ppermute(
        factors[0],
        "ad",
        [(z * N_X + x, (z + CHAIN) % n_z * N_X + x) for z in range(n_z) for x in range(N_X)],
    )

    def swap(array, mask):
        return lax.ppermute(array, "tp", [(j, j ^ mask) for j in range(n_tp)])

    def blocks(count, kind):
        return jax.ShapeDtypeStruct((count, tok_rows, columns), kind)

    much = pl.CostEstimate(flops=4 * 10**10, bytes_accessed=tokens.size, transcendentals=0)
    keep, out = call(base_kernel, (blocks(4, BF16), blocks(4, BF16)), handed, in_hbm(tokens), in_hbm(key_value_weight), cost=much)
    out_recv = swap(out, 1)
    parts, lane_ids = call(
        project,
        (
            jax.ShapeDtypeStruct((n_tp, doubled_rank // 2, rows), BF16),
            jax.ShapeDtypeStruct((8, rows), F32),
        ),
        recv,
        *factors,
        handed,
        out_recv,
    )
    parts = lax.all_to_all(parts, "tp", 0, 0, tiled=True)
    delta, mark = call(
        apply_up,
        (
            jax.ShapeDtypeStruct((rows, columns), BF16),
            jax.ShapeDtypeStruct((8, LANES), F32),
        ),
        parts,
        lane_ids,
        *factors,
        handed,
    )
    shares = call(pair_kernel, (blocks(1, F32),) + (blocks(1, BF16),) * 3, mark, keep, out_recv)
    shares = shares[:1] + tuple(
        swap(share, mask) for share, mask in zip(shares[1:], (6, 2, 4), strict=True)
    )
    back = lax.all_to_all(
        delta.reshape(n_z, cap, columns), "ad", 0, 0, axis_index_groups=along_z, tiled=True
    )
    base, select = call(
        ready_kernel,
        (
            jax.ShapeDtypeStruct((tok_rows, columns), F32),
            jax.ShapeDtypeStruct((tok_rows, rows), BF16),
        ),
        place,
        *shares,
        cost=pl.CostEstimate(flops=10**9, bytes_accessed=tokens.size, transcendentals=0),
    )
    return call(
        mix_kernel,
        jax.ShapeDtypeStruct((tok_rows, columns), BF16),
        back.reshape(rows, columns),
        base,
        select,
    )


def solution(mesh):
    return jax.shard_map(
        local,
        mesh=mesh,
        in_specs=(
            P("ad", "tp"),
            P("tp", None),
            P("ad", None, "tp"),
            P("ad", None, "tp"),
            P("ad"),
            P("ad", None),
        ),
        out_specs=P("ad", "tp"),
        check_vma=False,
    )
```

```python
import jax
import jax.numpy as jnp
from jax import lax
from jax.experimental import pallas as pl
from jax.experimental.pallas import tpu as pltpu
from jax.sharding import PartitionSpec as P

ADAPTER_SCALE = 2.0
N_X = 4
MAXLEN = 8
CHAIN = 1

F32 = jnp.float32
BF16 = jnp.bfloat16
NT = (((1,), (1,)), ((), ()))
TN = (((0,), (0,)), ((), ()))
LANES = 128
PIECES = 4
VMEM_LIMIT = 48 * 1024 * 1024


def iota(shape, dimension):
    return lax.broadcasted_iota(jnp.int32, shape, dimension)


def pack_kernel(
    planes, cap, stored,
    lens_hbm, index_hbm, tokens_hbm, down_hbm, up_hbm,
    send_hbm, place_ref, factors_hbm,
    lens_ref, index_ref, tokens_ref, block_ref, up_ref, send_ref, sems,
):
    requests = lens_ref.shape[1]
    rows, width = tokens_ref.shape
    adapters, rank, columns = up_ref.shape
    down_rows = down_hbm.shape[0]

    def copy(source, target, k):
        made = pltpu.make_async_copy(source, target, sems.at[k])
        made.start()
        return made

    get_lens = copy(lens_hbm, lens_ref, 0)
    get_index = copy(index_hbm, index_ref, 1)
    get_tokens = copy(tokens_hbm, tokens_ref, 2)
    get_down = copy(down_hbm, block_ref.at[pl.ds(0, down_rows)], 3)
    get_up = copy(up_hbm, up_ref, 4)

    get_lens.wait()
    get_index.wait()
    lens = lens_ref[...].astype(F32)
    index = index_ref[...].astype(F32)
    r0, r1 = iota((requests, requests), 0), iota((requests, requests), 1)
    ends = jnp.sum(jnp.where(r1 <= r0, lens, 0.0), axis=1, keepdims=True)
    starts = jnp.sum(jnp.where(r1 < r0, lens, 0.0), axis=1, keepdims=True)
    index_col = jnp.sum(jnp.where(r1 == r0, index, 0.0), axis=1, keepdims=True)
    owner = jnp.floor(index_col * (1.0 / stored))
    same_earlier = (owner == jnp.floor(index * (1.0 / stored))) & (r1 < r0)
    first = jnp.sum(jnp.where(same_earlier, 1.0, 0.0), axis=1, keepdims=True) == 0.0
    within = index_col - owner * stored
    home = jnp.floor(owner * (1.0 / N_X))
    column = owner - home * N_X
    lane = iota((requests, planes), 1).astype(F32)
    counts = jnp.sum(jnp.where(home == lane, 1.0, 0.0), axis=0, keepdims=True)
    number = lane[0:1]
    over = jnp.sum(jnp.where(counts > N_X, number, 0.0), axis=1, keepdims=True)
    under = jnp.sum(jnp.where(counts < N_X, number, 0.0), axis=1, keepdims=True)

    def ahead(steps):
        steps = steps * CHAIN
        return jnp.where(steps < 0.0, steps + planes, steps)

    my_x = lax.axis_index("ad") % N_X
    relative = (column.astype(jnp.int32) ^ my_x).astype(F32)
    in_chain = ahead(home - over) < ahead(under - over)
    handed = in_chain & first & (relative == 0.0)
    target = jnp.where(handed, home + CHAIN, home)
    target = jnp.where(target < 0.0, target + planes, target)
    target = jnp.where(target >= planes, target - planes, target)
    block = jnp.where(handed, float(N_X), relative) * stored + within
    t = iota((requests, rows), 1).astype(F32)
    inside = (t >= starts) & (t < ends)
    plane = jnp.sum(jnp.where(inside, target, 0.0), axis=0, keepdims=True)
    local = jnp.sum(jnp.where(inside, block, 0.0), axis=0, keepdims=True)
    member = iota((planes, rows), 0).astype(F32) == plane
    before = (iota((rows, rows), 0) < iota((rows, rows), 1)).astype(F32).astype(BF16)
    earlier = jnp.dot(member.astype(F32).astype(BF16), before, preferred_element_type=F32)
    rank_in = jnp.sum(jnp.where(member, earlier, 0.0), axis=0, keepdims=True)
    place = (plane * cap + rank_in).astype(jnp.int32)
    place_ref[...] = jnp.broadcast_to(place, place_ref.shape)
    select = (iota((planes * cap, rows), 0) == place).astype(F32).astype(BF16)

    get_up.wait()
    for a in range(adapters):
        pair, side = a // 2, a % 2
        block_ref[
            down_rows + pair * rank : down_rows + (pair + 1) * rank,
            side * columns : (side + 1) * columns,
        ] = up_ref[a]
    get_down.wait()
    put = copy(block_ref, factors_hbm, 5)

    get_tokens.wait()
    at_rank = (iota((LANES, rows), 0).astype(F32) == rank_in).astype(F32).astype(BF16)
    ids = lax.dot_general(
        jnp.where(member, local, 0.0).astype(BF16), at_rank, NT, preferred_element_type=F32
    )
    ids = jnp.broadcast_to(ids.reshape(planes, 1, LANES), (planes, 8, LANES))
    blocks = width // LANES
    send_ref[:, blocks * cap :, :] = ids.astype(BF16)
    sends = []
    part = planes // PIECES
    for k in range(PIECES):
        packed = jnp.dot(
            select[k * part * cap : (k + 1) * part * cap],
            tokens_ref[...],
            preferred_element_type=F32,
        )
        for c in range(blocks):
            block = packed[:, c * LANES : (c + 1) * LANES].reshape(part, cap, LANES)
            send_ref[k * part : (k + 1) * part, c * cap : (c + 1) * cap, :] = block.astype(BF16)
        piece = pl.ds(k * part, part)
        sends.append(copy(send_ref.at[piece], send_hbm.at[piece], 6 + k))
    for send in sends:
        send.wait()
    put.wait()


def base_kernel(place_ref, tokens_ref, weight_ref, keep_ref, send_ref):
    del place_ref
    columns = keep_ref.shape[2]
    me = lax.axis_index("tp")

    def block(relative):
        first = pl.multiple_of((me ^ relative) * columns, columns)
        return jnp.dot(
            tokens_ref[...], weight_ref[:, pl.ds(first, columns)], preferred_element_type=F32
        ).astype(BF16)

    for k, relative in enumerate((0, 6, 2, 4)):
        send_ref[k] = block(relative ^ 1)
        keep_ref[k] = block(relative)


def halve_kernel(after_ref, keep_ref, recv_ref, kept_ref, send_ref):
    del after_ref
    half = kept_ref.shape[0]
    for k in range(half):
        kept_ref[k] = keep_ref[k].astype(F32) + recv_ref[k].astype(F32)
        send_ref[k] = (keep_ref[half + k].astype(F32) + recv_ref[half + k].astype(F32)).astype(BF16)


def low_kernel(
    planes, cap, stored, recv_ref, f0_ref, f1_ref, f2_ref, f3_ref,
    handed_ref, kept_ref, out_ref, lane_ids_ref
):
    del kept_ref
    rows = planes * cap
    blocks = recv_ref.shape[1] // cap
    source = iota((planes, rows), 0)
    p = iota((planes, rows), 1)
    mine = (p >= source * cap) & (p < source * cap + cap)
    offset = jnp.sum(jnp.where(mine, p - source * cap, 0).astype(F32), axis=0, keepdims=True)
    spread = (iota((LANES, rows), 0).astype(F32) == offset).astype(F32).astype(BF16)
    ids = recv_ref[:, blocks * cap :, :].astype(F32)[:, 0, :].astype(BF16)
    ids = jnp.dot(ids, spread, preferred_element_type=F32)
    ids = jnp.sum(jnp.where(mine, ids, 0.0), axis=0, keepdims=True)
    lane_ids_ref[...] = jnp.broadcast_to(ids, lane_ids_ref.shape)
    recv = jnp.concatenate(
        [
            recv_ref[:, c * cap : (c + 1) * cap, :].astype(F32).reshape(rows, LANES).astype(BF16)
            for c in range(blocks)
        ],
        axis=1,
    )
    n, rank = out_ref.shape[:2]
    doubled = 2 * rank
    low = jnp.zeros((doubled, rows), F32)
    for x, factors_ref in enumerate((f0_ref, f1_ref, f2_ref, f3_ref, handed_ref)):
        block = factors_ref[: stored * doubled, :]
        values = lax.dot_general(block, recv, NT, preferred_element_type=F32)
        for a in range(stored):
            low = jnp.where(
                ids == float(x * stored + a), values[a * doubled : (a + 1) * doubled], low
            )
    low = low.astype(BF16)
    for j in range(n):
        half = j * 2 // n
        out_ref[j] = low[half * rank : (half + 1) * rank]


def delta_kernel(
    stored, parts_ref, lane_ids_ref, f0_ref, f1_ref, f2_ref, f3_ref,
    handed_ref, out_hbm, mark_ref, out_ref, sems
):
    low = parts_ref[0].astype(F32)
    for j in range(1, parts_ref.shape[0]):
        low = low + parts_ref[j].astype(F32)
    rank = low.shape[0]
    columns = out_ref.shape[1]
    ids = lane_ids_ref[0:1, :]
    spread, up = [], []
    for x, factors_ref in enumerate((f0_ref, f1_ref, f2_ref, f3_ref, handed_ref)):
        for side in range(2):
            up.append(factors_ref[stored * 2 * rank :, side * columns : (side + 1) * columns])
            for pair in range(stored // 2):
                a = float(x * stored + 2 * pair + side)
                spread.append(jnp.where(ids == a, low, 0.0).astype(BF16))
    spread = jnp.concatenate(spread, axis=0)
    up = jnp.concatenate(up, axis=0)
    part = out_ref.shape[0] // PIECES
    puts = []
    for k in range(PIECES):
        piece = slice(k * part, (k + 1) * part)
        product = lax.dot_general(spread[:, piece], up, TN, preferred_element_type=F32)
        out_ref[piece, :] = product.astype(BF16)
        puts.append(
            pltpu.make_async_copy(
                out_ref.at[pl.ds(k * part, part)], out_hbm.at[pl.ds(k * part, part)], sems.at[k]
            )
        )
        puts[-1].start()
    for put in puts:
        put.wait()
    mark_ref[...] = jnp.zeros(mark_ref.shape, F32)


def mix_kernel(place_ref, back_ref, kept_ref, recv_ref, out_ref):
    rows = out_ref.shape[0]
    place = place_ref[0:1, :]
    select = (iota((back_ref.shape[0], rows), 0) == place).astype(F32).astype(BF16)
    delta = lax.dot_general(select, back_ref[...], TN, preferred_element_type=F32)
    base = kept_ref[0] + recv_ref[0].astype(F32)
    out_ref[...] = (base + ADAPTER_SCALE * delta).astype(BF16)


def call(kernel, out_shape, *args, cost=None):
    return pl.pallas_call(
        kernel,
        out_shape=out_shape,
        compiler_params=pltpu.CompilerParams(vmem_limit_bytes=VMEM_LIMIT),
        cost_estimate=cost,
    )(*args)


def in_hbm(array):
    return pltpu.with_memory_space_constraint(array, pltpu.HBM)


def local(
    tokens, key_value_weight, adapter_down_weight, adapter_up_weight, request_adapter_index, lengths
):
    tok_rows, width = tokens.shape
    n_ad = lax.axis_size("ad")
    n_tp = lax.axis_size("tp")
    n_z = n_ad // N_X
    stored, doubled_rank, _ = adapter_down_weight.shape
    rank, columns = adapter_up_weight.shape[1:]
    cap = N_X * MAXLEN
    rows = n_z * cap
    along_x = [[z * N_X + x for x in range(N_X)] for z in range(n_z)]
    along_z = [[z * N_X + x for z in range(n_z)] for x in range(N_X)]

    def pack(*refs):
        pack_kernel(n_z, cap, stored, *refs)

    def project(*refs):
        low_kernel(n_z, cap, stored, *refs)

    def apply_up(*refs):
        delta_kernel(stored, *refs)

    hbm = pl.BlockSpec(memory_space=pltpu.HBM)
    vmem = pl.BlockSpec(memory_space=pltpu.VMEM)
    block_rows = stored * doubled_rank + stored // 2 * rank
    send, place, factors = pl.pallas_call(
        pack,
        out_shape=(
            jax.ShapeDtypeStruct((n_z, width // LANES * cap + 8, LANES), BF16),
            jax.ShapeDtypeStruct((8, tok_rows), jnp.int32),
            jax.ShapeDtypeStruct((block_rows, width), BF16),
        ),
        in_specs=[hbm] * 5,
        out_specs=(hbm, vmem, hbm),
        scratch_shapes=[
            pltpu.VMEM((1, lengths.shape[1]), jnp.int32),
            pltpu.VMEM((1, lengths.shape[1]), jnp.int32),
            pltpu.VMEM((tok_rows, width), BF16),
            pltpu.VMEM((block_rows, width), BF16),
            pltpu.VMEM((stored, rank, columns), BF16),
            pltpu.VMEM((n_z, width // LANES * cap + 8, LANES), BF16),
            pltpu.SemaphoreType.DMA((6 + PIECES,)),
        ],
        compiler_params=pltpu.CompilerParams(vmem_limit_bytes=VMEM_LIMIT),
    )(
        *(
            pltpu.with_memory_space_constraint(array, pltpu.HBM)
            for array in (
                lengths,
                request_adapter_index.reshape(1, -1),
                tokens,
                adapter_down_weight.reshape(stored * doubled_rank, width),
                adapter_up_weight,
            )
        )
    )
    recv = lax.all_to_all(send, "ad", 0, 0, axis_index_groups=along_z, tiled=True)
    factors = [factors] + [
        lax.ppermute(
            factors, "ad", [(z * N_X + x, z * N_X + (x ^ s)) for z in range(n_z) for x in range(N_X)]
        )
        for s in range(1, N_X)
    ]

    handed = lax.ppermute(
        factors[0],
        "ad",
        [(z * N_X + x, (z + CHAIN) % n_z * N_X + x) for z in range(n_z) for x in range(N_X)],
    )

    def swap(array, mask):
        return lax.ppermute(array, "tp", [(j, j ^ mask) for j in range(n_tp)])

    def blocks(count, kind):
        return jax.ShapeDtypeStruct((count, tok_rows, columns), kind)

    much = pl.CostEstimate(flops=4 * 10**10, bytes_accessed=tokens.size, transcendentals=0)
    keep, out = call(base_kernel, (blocks(4, BF16), blocks(4, BF16)), handed, in_hbm(tokens), in_hbm(key_value_weight), cost=much)
    out_recv = swap(out, 1)
    parts, lane_ids = call(
        project,
        (
            jax.ShapeDtypeStruct((n_tp, doubled_rank // 2, rows), BF16),
            jax.ShapeDtypeStruct((8, rows), F32),
        ),
        recv,
        *factors,
        handed,
        out_recv,
    )
    parts = lax.all_to_all(parts, "tp", 0, 0, tiled=True)
    delta, mark = pl.pallas_call(
        apply_up,
        out_shape=(
            jax.ShapeDtypeStruct((rows, columns), BF16),
            jax.ShapeDtypeStruct((8, LANES), F32),
        ),
        in_specs=[vmem] * 7,
        out_specs=(hbm, vmem),
        scratch_shapes=[
            pltpu.VMEM((rows, columns), BF16),
            pltpu.SemaphoreType.DMA((PIECES,)),
        ],
        compiler_params=pltpu.CompilerParams(vmem_limit_bytes=VMEM_LIMIT),
    )(parts, lane_ids, *factors, handed)
    keep, out = call(halve_kernel, (blocks(2, F32), blocks(2, BF16)), mark, keep, out_recv)
    keep, out = call(halve_kernel, (blocks(1, F32), blocks(1, BF16)), mark, keep, swap(out, 2))
    base_recv = swap(out, 6)
    back = lax.all_to_all(
        delta.reshape(n_z, cap, columns), "ad", 0, 0, axis_index_groups=along_z, tiled=True
    )
    return call(
        mix_kernel,
        jax.ShapeDtypeStruct((tok_rows, columns), BF16),
        place,
        back.reshape(rows, columns),
        keep,
        base_recv,
    )


def solution(mesh):
    return jax.shard_map(
        local,
        mesh=mesh,
        in_specs=(
            P("ad", "tp"),
            P("tp", None),
            P("ad", None, "tp"),
            P("ad", None, "tp"),
            P("ad"),
            P("ad", None),
        ),
        out_specs=P("ad", "tp"),
        check_vma=False,
    )
```
